512 devices in a mesh: seq: 128 (over x_lo, z, y), head: 4 (over x_hi, core).
Axes of the slice: x: 4 (x_hi: 2, x_lo: 2; x = x_hi * 2 + x_lo), y: 4, z: 16, core: 2. Of those that a mesh axis runs over, the one named last changes fastest.
Arguments:
- queries: bfloat16 [16384, 8192], P(('seq', 'head')), may hold values from -5 to 5
- output_gradient: bfloat16 [16384, 8192], P(('seq', 'head')), may hold values from -5 to 5
- response_key_value: bfloat16 [16384, 2, 1024], P(('seq', 'head')), may hold values from -5 to 5
- prompt_key_value: bfloat16 [2048, 2, 1024], P('seq', None, 'head'), may hold values from -5 to 5
- packing: int32 [128], replicated, may hold values from 0 to 127, each once
- lengths: int32 [128], replicated, may hold values from 1 to 128, as said below
- prompt_owner: int32 [128], replicated, may hold values from 0 to 127, each once
Outputs:
- query_grad: bfloat16 [16384, 8192], P(('seq', 'head'))
- resp_grad: bfloat16 [16384, 2, 1024], P(('seq', 'head'))
- prompt_grad: float32 [2048, 2, 1024], P('seq', None, 'head')
The draws below stay inside these ranges and needn't reach their ends.
Inputs may be any that keep to these rules, and one draw needn't show every extreme that they name: `packing`: every response is held by exactly one index of seq. `prompt_owner`: every index of seq holds exactly one prompt piece. `lengths`: some response fills all 128 slots.
All inputs are finite; a program needn't handle non-finite values.
Results may differ from the reference program's by a relative error of at most 0.0094.
Values may be sent and summed in bfloat16 or wider, within the bound.
No kernel may reach another device: no remote copies, remote signals or barrier semaphores. Data moves between devices by JAX's collectives and lax.ppermute only.
A program may use at most 64 MiB of HBM per device.

```python
import math
import jax
import jax.numpy as jnp
from jax import lax

QUERY_HEADS = 64
KEY_VALUE_HEADS = 8
HEAD_SIZE = 128
RESPONSE_SLOTS = 128
PIECE = 16
GROUP = 16
PROMPT_LENGTH = 256
RESPONSE_TOKENS = 16384
PROMPT_TOKEN_SUM = 2048
N_SEQ = 128


def draw_queries(key, part):
    key = jax.random.fold_in(key, 7)
    array_shape = (RESPONSE_TOKENS, QUERY_HEADS, HEAD_SIZE)
    base_offset = jnp.clip(jax.random.normal(key, array_shape, jnp.float32), -5.0, 5.0)
    return base_offset.reshape(RESPONSE_TOKENS, QUERY_HEADS * HEAD_SIZE).astype(jnp.bfloat16)


def draw_prompt_key_value(key, part):
    key = jax.random.fold_in(key, 8)
    array_shape = (PROMPT_TOKEN_SUM, 2, KEY_VALUE_HEADS, HEAD_SIZE)
    base_offset = jnp.clip(jax.random.normal(key, array_shape, jnp.float32), -5.0, 5.0)
    return base_offset.reshape(PROMPT_TOKEN_SUM, 2, KEY_VALUE_HEADS * HEAD_SIZE).astype(jnp.bfloat16)


def draw_lengths(key, part):
    key = jax.random.fold_in(key, 31)
    first_key, second_key = jax.random.split(key)
    base_offset = jax.random.randint(first_key, (N_SEQ,), 1, RESPONSE_SLOTS + 1)
    longest = jax.random.randint(second_key, (), 0, N_SEQ)
    return jnp.where(jnp.arange(N_SEQ) == longest, RESPONSE_SLOTS, base_offset).astype(jnp.int32)


def shard_levels(own_key, dims, cuts, low, largest):
    def one(axis_at, parts):
        steps = jax.random.uniform(jax.random.fold_in(jax.random.fold_in(own_key, 6), axis_at), (parts,), jnp.float32, low / len(cuts), largest / len(cuts))
        return jnp.repeat(jnp.exp(steps), dims[axis_at] // parts).reshape((-1,) + (1,) * (len(dims) - axis_at - 1))

    factor_of = one(*cuts[0])
    for cut in cuts[1:]:
        factor_of = factor_of * one(*cut)
    return factor_of


def bell_draw(rng, extent, width, bound, cuts=(), held_as=jnp.bfloat16):
    drawn = jax.random.normal(rng, extent, jnp.float32) * width
    if len(cuts) > 0:
        drawn = shard_levels(rng, extent, cuts, -0.22, 0.18) * drawn
    return jnp.clip(drawn, min=-bound, max=bound).astype(held_as)


def setup_inputs(seed: int = 0) -> dict:
    key_list = jax.random.split(jax.random.key(seed), 8)
    return {
        "queries": draw_queries(jax.random.fold_in(key_list[7], 71), 0),
        "output_gradient": bell_draw(key_list[1], (RESPONSE_TOKENS, QUERY_HEADS * HEAD_SIZE), 1.0, 5.0, ((0, 512),)),
        "response_key_value": bell_draw(key_list[2], (RESPONSE_TOKENS, 2, KEY_VALUE_HEADS * HEAD_SIZE), 1.0, 5.0, ((0, 512),)),
        "prompt_key_value": draw_prompt_key_value(jax.random.fold_in(key_list[7], 71), 0),
        "packing": jax.random.permutation(key_list[4], N_SEQ).astype(jnp.int32),
        "lengths": draw_lengths(jax.random.fold_in(key_list[7], 71), 0),
        "prompt_owner": jax.random.permutation(key_list[6], N_SEQ).astype(jnp.int32),
    }


def reference(queries, output_gradient, response_key_value, prompt_key_value, packing, lengths, prompt_owner):
    grouped_heads = QUERY_HEADS // KEY_VALUE_HEADS
    inv_root = 1.0 / math.sqrt(HEAD_SIZE)
    key_tally = PROMPT_LENGTH + RESPONSE_SLOTS
    offsets = jnp.arange(PIECE, dtype=jnp.int32)

    def one(running_totals, holder):
        response = packing[holder]
        length = lengths[response]
        prompt = response // GROUP
        owners = lax.dynamic_slice_in_dim(prompt_owner, (prompt * GROUP).astype(jnp.int32), GROUP)
        sender_rows = (owners[:, None] * PIECE + offsets[None, :]).reshape(PROMPT_LENGTH).astype(jnp.int32)
        first_entry = (holder * RESPONSE_SLOTS).astype(jnp.int32)
        query_row_block = lax.dynamic_slice_in_dim(queries, first_entry, RESPONSE_SLOTS, 0).astype(jnp.float32).reshape(RESPONSE_SLOTS, KEY_VALUE_HEADS, grouped_heads, HEAD_SIZE)
        gradient_row_block = lax.dynamic_slice_in_dim(output_gradient, first_entry, RESPONSE_SLOTS, 0).astype(jnp.float32).reshape(RESPONSE_SLOTS, KEY_VALUE_HEADS, grouped_heads, HEAD_SIZE)
        owned_rows = lax.dynamic_slice_in_dim(response_key_value, first_entry, RESPONSE_SLOTS, 0).astype(jnp.float32).reshape(RESPONSE_SLOTS, 2, KEY_VALUE_HEADS, HEAD_SIZE)
        prompt_row_block = prompt_key_value[sender_rows].astype(jnp.float32).reshape(PROMPT_LENGTH, 2, KEY_VALUE_HEADS, HEAD_SIZE)
        key_rows = jnp.concatenate([prompt_row_block[:, 0], owned_rows[:, 0]], axis=0)
        value_rows = jnp.concatenate([prompt_row_block[:, 1], owned_rows[:, 1]], axis=0)
        scores = jnp.einsum('igrd,kgd->igrk', query_row_block, key_rows) * inv_root
        query_pos = jnp.arange(RESPONSE_SLOTS, dtype=jnp.int32)[:, None, None, None]
        key_pos = jnp.arange(key_tally, dtype=jnp.int32)[None, None, None, :]
        valid = query_pos < length
        allowed = ((key_pos < PROMPT_LENGTH) | (key_pos - PROMPT_LENGTH <= query_pos)) & valid
        row_max = lax.optimization_barrier(jnp.max(jnp.where(allowed, scores, -jnp.inf), axis=-1, keepdims=True))
        row_max = jnp.where(valid, row_max, 0.0)
        exponent = jnp.where(allowed, jnp.exp(scores - row_max), 0.0)
        row_total = lax.optimization_barrier(jnp.sum(exponent, axis=-1, keepdims=True))
        weights = exponent / jnp.where(valid, row_total, 1.0)
        weight_half = lax.optimization_barrier(weights.astype(jnp.bfloat16)).astype(jnp.float32)
        outputs = jnp.einsum('igrk,kgd->igrd', weight_half, value_rows)
        delta = lax.optimization_barrier(jnp.sum(gradient_row_block * outputs, axis=-1, keepdims=True))
        dprob = jnp.einsum('igrd,kgd->igrk', gradient_row_block, value_rows)
        dscore_half = lax.optimization_barrier((weights * (dprob - delta)).astype(jnp.bfloat16)).astype(jnp.float32)
        query_grad = (jnp.einsum('igrk,kgd->igrd', dscore_half, key_rows) * inv_root).astype(jnp.bfloat16)
        key_gradient = jnp.einsum('igrk,igrd->kgd', dscore_half, query_row_block) * inv_root
        value_gradient = jnp.einsum('igrk,igrd->kgd', weight_half, gradient_row_block)
        gradient_result = jnp.stack([key_gradient, value_gradient], axis=1).reshape(key_tally, 2, KEY_VALUE_HEADS * HEAD_SIZE)
        running_totals = running_totals.at[sender_rows].add(gradient_result[:PROMPT_LENGTH])
        own_grad = gradient_result[PROMPT_LENGTH:].astype(jnp.bfloat16)
        return (running_totals, (query_grad.reshape(RESPONSE_SLOTS, QUERY_HEADS * HEAD_SIZE), own_grad))
    starting_totals = jnp.zeros((PROMPT_TOKEN_SUM, 2, KEY_VALUE_HEADS * HEAD_SIZE), jnp.float32)
    running_totals, (query_complete, owned_everything) = lax.scan(one, starting_totals, jnp.arange(N_SEQ, dtype=jnp.int32))
    return (query_complete.reshape(RESPONSE_TOKENS, QUERY_HEADS * HEAD_SIZE), owned_everything.reshape(RESPONSE_TOKENS, 2, KEY_VALUE_HEADS * HEAD_SIZE), running_totals)
```

```python
import math

import jax
import jax.numpy as jnp
from jax import lax
from jax.experimental import pallas as pl
from jax.experimental.pallas import tpu as pltpu
from jax.sharding import Mesh
from jax.sharding import PartitionSpec as P

QUERY_HEADS = 64
KEY_VALUE_HEADS = 8
HEAD = 128
GROUP = 16
PIECE = 16
PROMPT = GROUP * PIECE
SLOTS = 128
KEYS = PROMPT + SLOTS
X_LO, Z, Y = 2, 16, 4
PLANE = X_LO * Y
N_SEQ = PLANE * Z
N_HEAD = 4
LOCAL_ROWS = SLOTS // N_HEAD
KV_LOCAL = KEY_VALUE_HEADS // N_HEAD
PER_GROUP = QUERY_HEADS // KEY_VALUE_HEADS
Q_WIDTH = KV_LOCAL * PER_GROUP * HEAD
KV_WIDTH = KV_LOCAL * HEAD
IN_WIDTH = 2 * Q_WIDTH + 2 * KV_WIDTH
OUT_WIDTH = Q_WIDTH + 2 * KV_WIDTH
INV_ROOT = 1.0 / math.sqrt(HEAD)
EXP2_SCALE = INV_ROOT / math.log(2.0)

BF16 = jnp.bfloat16
F32 = jnp.float32
SMEM = pl.BlockSpec(memory_space=pltpu.SMEM)
VMEM = pl.BlockSpec(memory_space=pltpu.VMEM)


def params(mib):
    return pltpu.CompilerParams(vmem_limit_bytes=mib * 2**20)


def dot(a, b, contract):
    return lax.dot_general(a, b, (contract, ((), ())), preferred_element_type=F32)


def spread_kernel(piece_ref, out_ref):
    flat = jnp.concatenate([piece_ref[:, 0, :], piece_ref[:, 1, :]], axis=1)
    for z in range(Z):
        out_ref[z] = flat


def spread_piece(piece):
    return pl.pallas_call(
        spread_kernel,
        out_shape=jax.ShapeDtypeStruct((Z, PIECE, 2 * KV_WIDTH), BF16),
        in_specs=[VMEM],
        out_specs=VMEM,
        compiler_params=params(16),
    )(piece)


def pack_kernel(q_ref, g_ref, kv_ref, out_ref):
    out_ref[0, :, :Q_WIDTH] = q_ref[...]
    out_ref[0, :, Q_WIDTH : 2 * Q_WIDTH] = g_ref[...]
    out_ref[0, :, 2 * Q_WIDTH : 2 * Q_WIDTH + KV_WIDTH] = kv_ref[:, 0, :]
    out_ref[0, :, 2 * Q_WIDTH + KV_WIDTH :] = kv_ref[:, 1, :]


def pack_rows(queries, grads, kv):
    return pl.pallas_call(
        pack_kernel,
        grid=(N_HEAD,),
        out_shape=jax.ShapeDtypeStruct((N_HEAD, LOCAL_ROWS, IN_WIDTH), BF16),
        in_specs=[
            pl.BlockSpec((LOCAL_ROWS, Q_WIDTH), lambda h: (0, h)),
            pl.BlockSpec((LOCAL_ROWS, Q_WIDTH), lambda h: (0, h)),
            pl.BlockSpec((LOCAL_ROWS, 2, KV_WIDTH), lambda h: (0, 0, h)),
        ],
        out_specs=pl.BlockSpec((1, LOCAL_ROWS, IN_WIDTH), lambda h: (h, 0, 0)),
        compiler_params=params(16),
    )(queries, grads, kv)


def unpack_kernel(in_ref, q_ref, kv_ref):
    q_ref[...] = in_ref[0, :, :Q_WIDTH]
    kv_ref[:, 0, :] = in_ref[0, :, Q_WIDTH : Q_WIDTH + KV_WIDTH]
    kv_ref[:, 1, :] = in_ref[0, :, Q_WIDTH + KV_WIDTH :]


def unpack_rows(back):
    return pl.pallas_call(
        unpack_kernel,
        grid=(N_HEAD,),
        out_shape=(
            jax.ShapeDtypeStruct((LOCAL_ROWS, N_HEAD * Q_WIDTH), BF16),
            jax.ShapeDtypeStruct((LOCAL_ROWS, 2, N_HEAD * KV_WIDTH), BF16),
        ),
        in_specs=[pl.BlockSpec((1, LOCAL_ROWS, OUT_WIDTH), lambda h: (h, 0, 0))],
        out_specs=(
            pl.BlockSpec((LOCAL_ROWS, Q_WIDTH), lambda h: (0, h)),
            pl.BlockSpec((LOCAL_ROWS, 2, KV_WIDTH), lambda h: (0, 0, h)),
        ),
        compiler_params=params(16),
    )(back)


def sum_plane_kernel(in_ref, out_ref):
    total = in_ref[0].astype(F32)
    for i in range(1, PLANE):
        total += in_ref[i].astype(F32)
    out_ref[...] = total.astype(BF16)


def sum_plane(parts):
    return pl.pallas_call(
        sum_plane_kernel,
        out_shape=jax.ShapeDtypeStruct((Z * PIECE, 2 * KV_WIDTH), BF16),
        in_specs=[VMEM],
        out_specs=VMEM,
        compiler_params=params(16),
    )(parts)


def sum_line_kernel(in_ref, out_ref):
    total = in_ref[0].astype(F32)
    for i in range(1, Z):
        total += in_ref[i].astype(F32)
    out_ref[:, 0, :] = total[:, :KV_WIDTH]
    out_ref[:, 1, :] = total[:, KV_WIDTH:]


def sum_line(parts):
    return pl.pallas_call(
        sum_line_kernel,
        out_shape=jax.ShapeDtypeStruct((PIECE, 2, KV_WIDTH), F32),
        in_specs=[VMEM],
        out_specs=VMEM,
        compiler_params=params(16),
    )(parts)


def rows_of(ref, lo):
    return ref[:, :, lo : lo + HEAD].reshape(SLOTS, HEAD)


def attention_kernel(
    pos_ref, packing_ref, lengths_ref, owner_ref, rows_ref, pieces_ref,
    back_ref, grads_ref, key_ref, value_ref, weight_ref, dscore_ref,
):
    response = packing_ref[pos_ref[0]]
    length = lengths_ref[response]
    first = (response // GROUP) * GROUP
    places = []
    for j in range(GROUP):
        s = owner_ref[first + j]
        places.append(((s // (Z * Y)) * Y + s % Y) * Z + (s // Y) % Z)
    for j in range(GROUP):
        piece = pieces_ref[places[j]]
        key_ref[j * PIECE : (j + 1) * PIECE, :] = piece[:, :KV_WIDTH]
        value_ref[j * PIECE : (j + 1) * PIECE, :] = piece[:, KV_WIDTH:]
    for g in range(KV_LOCAL):
        cols = slice(g * HEAD, (g + 1) * HEAD)
        key_ref[PROMPT:, cols] = rows_of(rows_ref, 2 * Q_WIDTH + g * HEAD)
        value_ref[PROMPT:, cols] = rows_of(rows_ref, 2 * Q_WIDTH + KV_WIDTH + g * HEAD)
    grads_ref[...] = jnp.zeros_like(grads_ref)

    pair = 2
    width = pair * SLOTS
    query_pos = lax.broadcasted_iota(jnp.int32, (SLOTS, width), 1) % SLOTS
    causal = lax.broadcasted_iota(jnp.int32, (SLOTS, width), 0) <= query_pos
    used = query_pos[:1] < length

    for g in range(KV_LOCAL):
        cols = slice(g * HEAD, (g + 1) * HEAD)
        keys, values = key_ref[:, cols], value_ref[:, cols]
        queries, out_grads = [], []
        for c in range(PER_GROUP // pair):
            at = [(g * PER_GROUP + c * pair + i) * HEAD for i in range(pair)]
            query = jnp.concatenate([rows_of(rows_ref, lo) for lo in at], axis=0)
            out_grad = jnp.concatenate([rows_of(rows_ref, Q_WIDTH + lo) for lo in at], axis=0)
            queries.append(query)
            out_grads.append(out_grad)
            score = dot(keys, query, ((1,), (1,)))
            score = jnp.concatenate(
                [score[:PROMPT], jnp.where(causal, score[PROMPT:], -jnp.inf)], axis=0
            )
            top = jnp.max(score, axis=0, keepdims=True)
            raised = jnp.exp2((score - top) * EXP2_SCALE)
            total = jnp.sum(raised, axis=0, keepdims=True)
            weight = raised * jnp.where(used, 1.0 / total, 0.0)
            weight_half = weight.astype(BF16)
            dprob = dot(values, out_grad, ((1,), (1,)))
            delta = jnp.sum(weight_half.astype(F32) * dprob, axis=0, keepdims=True)
            dscore = (weight * (dprob - delta)).astype(BF16)
            weight_ref[:, c * width : (c + 1) * width] = weight_half
            dscore_ref[:, c * width : (c + 1) * width] = dscore
            query_grad = dot(keys, dscore, ((0,), (0,))).T * INV_ROOT
            for i, lo in enumerate(at):
                block = query_grad[i * SLOTS : (i + 1) * SLOTS].astype(BF16)
                back_ref[:, :, lo : lo + HEAD] = block.reshape(N_HEAD, LOCAL_ROWS, HEAD)
        key_grad = dot(dscore_ref[...], jnp.concatenate(queries, axis=0), ((1,), (0,))) * INV_ROOT
        value_grad = dot(weight_ref[...], jnp.concatenate(out_grads, axis=0), ((1,), (0,)))
        for slot, grad in enumerate((key_grad, value_grad)):
            grad = grad.astype(BF16)
            lo = slot * KV_WIDTH + g * HEAD
            for j in range(GROUP):
                grads_ref[places[j], :, lo : lo + HEAD] = grad[j * PIECE : (j + 1) * PIECE]
            back_ref[:, :, Q_WIDTH + lo : Q_WIDTH + lo + HEAD] = grad[PROMPT:].reshape(
                N_HEAD, LOCAL_ROWS, HEAD
            )


def attention(pos, packing, lengths, owner, rows, pieces):
    flops = 2 * 5 * KEYS * Q_WIDTH // HEAD * SLOTS * HEAD
    return pl.pallas_call(
        attention_kernel,
        out_shape=(
            jax.ShapeDtypeStruct((N_HEAD, LOCAL_ROWS, OUT_WIDTH), BF16),
            jax.ShapeDtypeStruct((N_SEQ, PIECE, 2 * KV_WIDTH), BF16),
        ),
        in_specs=[SMEM, SMEM, SMEM, SMEM, VMEM, VMEM],
        out_specs=(VMEM, VMEM),
        scratch_shapes=[
            pltpu.VMEM((KEYS, KV_WIDTH), BF16),
            pltpu.VMEM((KEYS, KV_WIDTH), BF16),
            pltpu.VMEM((KEYS, PER_GROUP * SLOTS), BF16),
            pltpu.VMEM((KEYS, PER_GROUP * SLOTS), BF16),
        ],
        compiler_params=params(32),
        cost_estimate=pl.CostEstimate(
            flops=flops, bytes_accessed=6 * 2**20, transcendentals=KEYS * SLOTS * 16
        ),
    )(pos, packing, lengths, owner, rows, pieces)


def exchange(parts, axes):
    return lax.all_to_all(parts, axes, split_axis=0, concat_axis=0, tiled=True)


def shards(queries, out_grads, response_kv, prompt_kv, packing, lengths, owner):
    position = lax.axis_index(("xl", "z", "y")).astype(jnp.int32).reshape(1)
    line = exchange(spread_piece(prompt_kv), "z")
    line = line.reshape(Z * PIECE, 2 * KV_WIDTH)
    pieces = exchange(jnp.broadcast_to(line[None], (PLANE,) + line.shape), ("xl", "y"))
    rows = exchange(pack_rows(queries, out_grads, response_kv), ("xh", "c"))
    back, grads = attention(
        position, packing, lengths, owner, rows, pieces.reshape(N_SEQ, PIECE, 2 * KV_WIDTH)
    )
    grads = exchange(grads.reshape(PLANE, Z * PIECE, 2 * KV_WIDTH), ("xl", "y"))
    grads = exchange(sum_plane(grads).reshape(Z, PIECE, 2 * KV_WIDTH), "z")
    query_grad, resp_grad = unpack_rows(exchange(back, ("xh", "c")))
    return query_grad, resp_grad, sum_line(grads)


def solution(mesh):
    fine = Mesh(mesh.devices.reshape(X_LO, Z, Y, 2, 2), ("xl", "z", "y", "xh", "c"))
    seq, head = ("xl", "z", "y"), ("xh", "c")
    return jax.shard_map(
        shards,
        mesh=fine,
        in_specs=(
            P(seq + head, None),
            P(seq + head, None),
            P(seq + head, None, None),
            P(seq, None, head),
            P(),
            P(),
            P(),
        ),
        out_specs=(
            P(seq + head, None),
            P(seq + head, None, None),
            P(seq, None, head),
        ),
        check_vma=False,
    )
```

```python
import functools
import math

import jax
import jax.numpy as jnp
from jax import lax
from jax.experimental import pallas as pl
from jax.experimental.pallas import tpu as pltpu
from jax.sharding import Mesh
from jax.sharding import PartitionSpec as P

QUERY_HEADS = 64
KEY_VALUE_HEADS = 8
HEAD = 128
GROUP = 16
PIECE = 16
PROMPT = GROUP * PIECE
SLOTS = 128
KEYS = PROMPT + SLOTS
X_LO, Z, Y = 2, 16, 4
PLANE = X_LO * Y
N_SEQ = PLANE * Z
SLOT_COUNTS = (5, 6, 8, GROUP)
PLANE_IN, PLANE_OUT = (3,), (1,)
N_HEAD = 4
LOCAL_ROWS = SLOTS // N_HEAD
KV_LOCAL = KEY_VALUE_HEADS // N_HEAD
PER_GROUP = QUERY_HEADS // KEY_VALUE_HEADS
Q_WIDTH = KV_LOCAL * PER_GROUP * HEAD
KV_WIDTH = KV_LOCAL * HEAD
IN_WIDTH = 2 * Q_WIDTH + 2 * KV_WIDTH
OUT_WIDTH = Q_WIDTH + 2 * KV_WIDTH
INV_ROOT = 1.0 / math.sqrt(HEAD)
EXP2_SCALE = INV_ROOT / math.log(2.0)

BF16 = jnp.bfloat16
F32 = jnp.float32
PLACE, SOURCE, COUNT, CHOICE = range(4)

SMEM = pl.BlockSpec(memory_space=pltpu.SMEM)
VMEM = pl.BlockSpec(memory_space=pltpu.VMEM)


def params(mib):
    return pltpu.CompilerParams(vmem_limit_bytes=mib * 2**20)


def dot(a, b, contract):
    return lax.dot_general(a, b, (contract, ((), ())), preferred_element_type=F32)


def line_of(s):
    return ((s >> 6) << 2) | (s & 3)


def height_of(s):
    return (s >> 2) & 15


def plan_kernel(place_ref, packing_ref, owner_ref, plan_ref):
    me = place_ref[0]
    square = (N_SEQ, N_SEQ)
    lane = lax.broadcasted_iota(jnp.int32, square, 1)
    row = lax.broadcasted_iota(jnp.int32, square, 0)
    across = jnp.broadcast_to(owner_ref[...], square)
    down = across.T
    same = (line_of(down) == line_of(across)) & ((row >> 4) == (lane >> 4))
    ones = same.astype(jnp.int32)
    most = jnp.max(jnp.sum(ones, axis=0, keepdims=True), axis=1, keepdims=True)
    rank = jnp.sum(jnp.where(row < lane, ones, 0), axis=0, keepdims=True)
    plan_ref[PLACE : PLACE + 1, :] = line_of(owner_ref[...]) * GROUP + rank
    rank_down = jnp.sum(jnp.where(lane < row, ones, 0), axis=1, keepdims=True)
    wanted = jnp.zeros((1, N_SEQ), jnp.int32)
    for d in range(PLANE):
        there = (d // Y) * (Z * Y) + height_of(me) * Y + d % Y
        wanted = jnp.where((lane[:1] >> 4) == d, packing_ref[there] >> 4, wanted)
    held = ((row >> 4) == wanted) & (line_of(down) == line_of(me))
    found = held & (rank_down == (lane & 15))
    plan_ref[SOURCE : SOURCE + 1, :] = jnp.sum(
        jnp.where(found, height_of(down), 0), axis=0, keepdims=True
    )
    plan_ref[COUNT : COUNT + 1, :] = jnp.sum(held.astype(jnp.int32), axis=0, keepdims=True)
    choice = sum((most > n).astype(jnp.int32) for n in SLOT_COUNTS[:-1])
    plan_ref[CHOICE : CHOICE + 1, :] = jnp.broadcast_to(choice, (1, N_SEQ))


def make_plan(place, packing, owner):
    return pl.pallas_call(
        plan_kernel,
        out_shape=jax.ShapeDtypeStruct((4, N_SEQ), jnp.int32),
        in_specs=[SMEM, SMEM, VMEM],
        out_specs=VMEM,
    )(place, packing, owner.reshape(1, N_SEQ))


def select_kernel(slots, plan_ref, line_ref, out_ref):
    for d in range(PLANE):

        @pl.loop(0, plan_ref[COUNT, d * GROUP])
        def _(c, d=d):
            out_ref[d * slots + c] = line_ref[plan_ref[SOURCE, d * GROUP + c]]


def select(plan, line, slots):
    out = pl.pallas_call(
        functools.partial(select_kernel, slots),
        out_shape=jax.ShapeDtypeStruct((PLANE * slots, PIECE, 2 * KV_WIDTH), BF16),
        in_specs=[SMEM, VMEM],
        out_specs=VMEM,
        compiler_params=params(16),
    )(plan, line)
    return out.reshape(PLANE, slots * PIECE, 2 * KV_WIDTH)


def spread_kernel(piece_ref, out_ref):
    flat = jnp.concatenate([piece_ref[:, 0, :], piece_ref[:, 1, :]], axis=1)
    for z in range(Z):
        out_ref[z] = flat


def spread_piece(piece):
    return pl.pallas_call(
        spread_kernel,
        out_shape=jax.ShapeDtypeStruct((Z, PIECE, 2 * KV_WIDTH), BF16),
        in_specs=[VMEM],
        out_specs=VMEM,
        compiler_params=params(16),
    )(piece)


def pack_kernel(place_ref, q_ref, g_ref, kv_ref, *out_refs):
    for k, out_ref in enumerate(out_refs):
        other = place_ref[1] ^ k
        wide = pl.ds(pl.multiple_of(other * Q_WIDTH, Q_WIDTH), Q_WIDTH)
        narrow = pl.ds(pl.multiple_of(other * KV_WIDTH, KV_WIDTH), KV_WIDTH)
        out_ref[:, :Q_WIDTH] = q_ref[:, wide]
        out_ref[:, Q_WIDTH : 2 * Q_WIDTH] = g_ref[:, wide]
        out_ref[:, 2 * Q_WIDTH : 2 * Q_WIDTH + KV_WIDTH] = kv_ref[:, 0, narrow]
        out_ref[:, 2 * Q_WIDTH + KV_WIDTH :] = kv_ref[:, 1, narrow]


def pack_rows(place, queries, grads, kv):
    block = jax.ShapeDtypeStruct((LOCAL_ROWS, IN_WIDTH), BF16)
    return pl.pallas_call(
        pack_kernel,
        out_shape=(block,) * N_HEAD,
        in_specs=[SMEM, VMEM, VMEM, VMEM],
        out_specs=(VMEM,) * N_HEAD,
        compiler_params=params(16),
    )(place, queries, grads, kv)


def unpack_kernel(place_ref, *refs):
    q_ref, kv_ref = refs[N_HEAD:]
    for k, in_ref in enumerate(refs[:N_HEAD]):
        other = place_ref[1] ^ k
        wide = pl.ds(pl.multiple_of(other * Q_WIDTH, Q_WIDTH), Q_WIDTH)
        narrow = pl.ds(pl.multiple_of(other * KV_WIDTH, KV_WIDTH), KV_WIDTH)
        q_ref[:, wide] = in_ref[:, :Q_WIDTH]
        kv_ref[:, 0, narrow] = in_ref[:, Q_WIDTH : Q_WIDTH + KV_WIDTH]
        kv_ref[:, 1, narrow] = in_ref[:, Q_WIDTH + KV_WIDTH :]


def unpack_rows(place, blocks):
    return pl.pallas_call(
        unpack_kernel,
        out_shape=(
            jax.ShapeDtypeStruct((LOCAL_ROWS, N_HEAD * Q_WIDTH), BF16),
            jax.ShapeDtypeStruct((LOCAL_ROWS, 2, N_HEAD * KV_WIDTH), BF16),
        ),
        in_specs=[SMEM] + [VMEM] * N_HEAD,
        out_specs=(VMEM, VMEM),
        compiler_params=params(16),
    )(place, *blocks)


def sum_plane_kernel(slots, plan_ref, part_ref, out_ref, total_ref):
    total_ref[...] = jnp.zeros_like(total_ref)
    for d in range(PLANE):

        @pl.loop(0, plan_ref[COUNT, d * GROUP])
        def _(c, d=d):
            z = plan_ref[SOURCE, d * GROUP + c]
            total_ref[z] = total_ref[z] + part_ref[d * slots + c].astype(F32)

    out_ref[...] = total_ref[...].astype(BF16)


def sum_plane(plan, parts, slots):
    shape = (Z, PIECE, 2 * KV_WIDTH)
    return pl.pallas_call(
        functools.partial(sum_plane_kernel, slots),
        out_shape=jax.ShapeDtypeStruct(shape, BF16),
        in_specs=[SMEM, VMEM],
        out_specs=VMEM,
        scratch_shapes=[pltpu.VMEM(shape, F32)],
        compiler_params=params(16),
    )(plan, parts.reshape(PLANE * slots, PIECE, 2 * KV_WIDTH))


def sum_line_kernel(in_ref, out_ref):
    total = in_ref[0].astype(F32)
    for i in range(1, Z):
        total += in_ref[i].astype(F32)
    out_ref[:, 0, :] = total[:, :KV_WIDTH]
    out_ref[:, 1, :] = total[:, KV_WIDTH:]


def sum_line(parts):
    return pl.pallas_call(
        sum_line_kernel,
        out_shape=jax.ShapeDtypeStruct((PIECE, 2, KV_WIDTH), F32),
        in_specs=[VMEM],
        out_specs=VMEM,
        compiler_params=params(16),
    )(parts)


def slot_index(shape, dim, head):
    row = lax.broadcasted_iota(jnp.int32, shape, dim) % SLOTS
    return ((row // LOCAL_ROWS) ^ head) * LOCAL_ROWS + row % LOCAL_ROWS


def attention_kernel(slots, place_ref, packing_ref, lengths_ref, plan_ref, *refs):
    row_refs, pieces_ref, refs = refs[:N_HEAD], refs[N_HEAD], refs[N_HEAD + 1 :]
    back_refs, grads_ref, refs = refs[:N_HEAD], refs[N_HEAD], refs[N_HEAD + 1 :]
    key_ref, value_ref, weight_ref, dscore_ref = refs

    def rows_of(lo):
        return jnp.concatenate([ref[:, lo : lo + HEAD] for ref in row_refs], axis=0)

    def give_back(block, lo):
        for k, ref in enumerate(back_refs):
            ref[:, lo : lo + HEAD] = block[k * LOCAL_ROWS : (k + 1) * LOCAL_ROWS]

    response = packing_ref[place_ref[0]]
    length = lengths_ref[response]
    first = (response // GROUP) * GROUP
    places = []
    for j in range(GROUP):
        place = plan_ref[PLACE, first + j]
        places.append((place >> 4) * slots + (place & 15))
    for j, at in enumerate(places):
        piece = pieces_ref[at]
        key_ref[j * PIECE : (j + 1) * PIECE, :] = piece[:, :KV_WIDTH]
        value_ref[j * PIECE : (j + 1) * PIECE, :] = piece[:, KV_WIDTH:]
    for g in range(KV_LOCAL):
        cols = slice(g * HEAD, (g + 1) * HEAD)
        key_ref[PROMPT:, cols] = rows_of(2 * Q_WIDTH + g * HEAD)
        value_ref[PROMPT:, cols] = rows_of(2 * Q_WIDTH + KV_WIDTH + g * HEAD)

    pair = 2
    width = pair * SLOTS
    head = place_ref[1]
    query_pos = slot_index((1, width), 1, head)
    causal = slot_index((SLOTS, 1), 0, head) <= query_pos
    used = query_pos < length

    for g in range(KV_LOCAL):
        cols = slice(g * HEAD, (g + 1) * HEAD)
        keys, values = key_ref[:, cols], value_ref[:, cols]
        queries, out_grads = [], []
        for c in range(PER_GROUP // pair):
            at = [(g * PER_GROUP + c * pair + i) * HEAD for i in range(pair)]
            query = jnp.concatenate([rows_of(lo) for lo in at], axis=0)
            out_grad = jnp.concatenate([rows_of(Q_WIDTH + lo) for lo in at], axis=0)
            queries.append(query)
            out_grads.append(out_grad)
            score = dot(keys, query, ((1,), (1,)))
            score = jnp.concatenate(
                [score[:PROMPT], jnp.where(causal, score[PROMPT:], -jnp.inf)], axis=0
            )
            top = jnp.max(score, axis=0, keepdims=True)
            raised = jnp.exp2((score - top) * EXP2_SCALE)
            total = jnp.sum(raised, axis=0, keepdims=True)
            weight = raised * jnp.where(used, 1.0 / total, 0.0)
            weight_half = weight.astype(BF16)
            dprob = dot(values, out_grad, ((1,), (1,)))
            delta = jnp.sum(weight_half.astype(F32) * dprob, axis=0, keepdims=True)
            dscore = (weight * (dprob - delta)).astype(BF16)
            weight_ref[:, c * width : (c + 1) * width] = weight_half
            dscore_ref[:, c * width : (c + 1) * width] = dscore
            query_grad = dot(keys, dscore, ((0,), (0,))).T * INV_ROOT
            for i, lo in enumerate(at):
                give_back(query_grad[i * SLOTS : (i + 1) * SLOTS].astype(BF16), lo)
        key_grad = dot(dscore_ref[...], jnp.concatenate(queries, axis=0), ((1,), (0,))) * INV_ROOT
        value_grad = dot(weight_ref[...], jnp.concatenate(out_grads, axis=0), ((1,), (0,)))
        for slot, grad in enumerate((key_grad, value_grad)):
            grad = grad.astype(BF16)
            lo = slot * KV_WIDTH + g * HEAD
            for j, at in enumerate(places):
                grads_ref[at, :, lo : lo + HEAD] = grad[j * PIECE : (j + 1) * PIECE]
            give_back(grad[PROMPT:], Q_WIDTH + lo)


def attention(place, packing, lengths, plan, rows, pieces, slots):
    flops = 2 * 5 * KEYS * Q_WIDTH // HEAD * SLOTS * HEAD
    block = jax.ShapeDtypeStruct((LOCAL_ROWS, OUT_WIDTH), BF16)
    part = jax.ShapeDtypeStruct((PLANE * slots, PIECE, 2 * KV_WIDTH), BF16)
    out = pl.pallas_call(
        functools.partial(attention_kernel, slots),
        out_shape=(block,) * N_HEAD + (part,),
        in_specs=[SMEM] * 4 + [VMEM] * (N_HEAD + 1),
        out_specs=(VMEM,) * (N_HEAD + 1),
        scratch_shapes=[
            pltpu.VMEM((KEYS, KV_WIDTH), BF16),
            pltpu.VMEM((KEYS, KV_WIDTH), BF16),
            pltpu.VMEM((KEYS, PER_GROUP * SLOTS), BF16),
            pltpu.VMEM((KEYS, PER_GROUP * SLOTS), BF16),
        ],
        compiler_params=params(32),
        cost_estimate=pl.CostEstimate(
            flops=flops, bytes_accessed=6 * 2**20, transcendentals=KEYS * SLOTS * 16
        ),
    )(place, packing, lengths, plan, *rows, pieces.reshape(part.shape))
    return out[:N_HEAD], out[N_HEAD].reshape(PLANE, slots * PIECE, 2 * KV_WIDTH)


def exchange(parts, axes):
    return lax.all_to_all(parts, axes, split_axis=0, concat_axis=0, tiled=True)


def swap(blocks, which):
    return [
        lax.ppermute(block, ("xh", "c"), [(i, i ^ k) for i in range(N_HEAD)])
        if k in which
        else block
        for k, block in enumerate(blocks)
    ]


def shards(queries, out_grads, response_kv, prompt_kv, packing, lengths, owner):
    place = jnp.stack([lax.axis_index(("xl", "z", "y")), lax.axis_index(("xh", "c"))])
    place = place.astype(jnp.int32)
    plane = ("xl", "y")
    others = set(range(1, N_HEAD))
    line = exchange(spread_piece(prompt_kv), "z")
    plan = make_plan(place, packing, owner)
    rows = pack_rows(place, queries, out_grads, response_kv)
    rows = swap(rows, others - set(PLANE_IN))

    def backward(slots, plan, line, *rows):
        pieces = exchange(select(plan, line, slots), plane)
        rows = swap(rows, PLANE_IN)
        back, grads = attention(place, packing, lengths, plan, rows, pieces, slots)
        grads = exchange(grads, plane)
        return swap(back, PLANE_OUT), sum_plane(plan, grads, slots)

    back, grads = lax.switch(
        plan[CHOICE, 0],
        [functools.partial(backward, slots) for slots in SLOT_COUNTS],
        plan, line, *rows,
    )
    grads = exchange(grads, "z")
    back = swap(back, others - set(PLANE_OUT))
    query_grad, resp_grad = unpack_rows(place, back)
    return query_grad, resp_grad, sum_line(grads)


def solution(mesh):
    fine = Mesh(mesh.devices.reshape(X_LO, Z, Y, 2, 2), ("xl", "z", "y", "xh", "c"))
    seq, head = ("xl", "z", "y"), ("xh", "c")
    return jax.shard_map(
        shards,
        mesh=fine,
        in_specs=(
            P(seq + head, None),
            P(seq + head, None),
            P(seq + head, None, None),
            P(seq, None, head),
            P(),
            P(),
            P(),
        ),
        out_specs=(
            P(seq + head, None),
            P(seq + head, None, None),
            P(seq, None, head),
        ),
        check_vma=False,
    )
```

```python
import functools
import math

import jax
import jax.numpy as jnp
from jax import lax
from jax.experimental import pallas as pl
from jax.experimental.pallas import tpu as pltpu
from jax.sharding import Mesh
from jax.sharding import PartitionSpec as P

QUERY_HEADS = 64
KEY_VALUE_HEADS = 8
HEAD = 128
GROUP = 16
PIECE = 16
PROMPT = GROUP * PIECE
SLOTS = 128
KEYS = PROMPT + SLOTS
X_LO, Z, Y = 2, 16, 4
PLANE = X_LO * Y
N_SEQ = PLANE * Z
SLOT_COUNTS = (4, 5, 6, 7, 8, GROUP)
N_HEAD = 4
LOCAL_ROWS = SLOTS // N_HEAD
KV_LOCAL = KEY_VALUE_HEADS // N_HEAD
PER_GROUP = QUERY_HEADS // KEY_VALUE_HEADS
Q_WIDTH = KV_LOCAL * PER_GROUP * HEAD
KV_WIDTH = KV_LOCAL * HEAD
IN_WIDTH = 2 * Q_WIDTH + 2 * KV_WIDTH
OUT_WIDTH = Q_WIDTH + 2 * KV_WIDTH
CHUNK, STRIP = 8, 64
INV_ROOT = 1.0 / math.sqrt(HEAD)
EXP2_SCALE = INV_ROOT / math.log(2.0)

BF16 = jnp.bfloat16
F32 = jnp.float32
PLACE, SOURCE, COUNT, CHOICE = range(4)

SMEM = pl.BlockSpec(memory_space=pltpu.SMEM)
VMEM = pl.BlockSpec(memory_space=pltpu.VMEM)


def params(mib):
    return pltpu.CompilerParams(vmem_limit_bytes=mib * 2**20)


def dot(a, b, contract):
    return lax.dot_general(a, b, (contract, ((), ())), preferred_element_type=F32)


def line_of(s):
    return ((s >> 6) << 2) | (s & 3)


def height_of(s):
    return (s >> 2) & 15


def plan_kernel(place_ref, packing_ref, owner_ref, plan_ref):
    me = place_ref[0]
    square = (N_SEQ, N_SEQ)
    lane = lax.broadcasted_iota(jnp.int32, square, 1)
    row = lax.broadcasted_iota(jnp.int32, square, 0)
    across = jnp.broadcast_to(owner_ref[...], square)
    down = across.T
    same = (line_of(down) == line_of(across)) & ((row >> 4) == (lane >> 4))
    ones = same.astype(jnp.int32)
    most = jnp.max(jnp.sum(ones, axis=0, keepdims=True), axis=1, keepdims=True)
    rank = jnp.sum(jnp.where(row < lane, ones, 0), axis=0, keepdims=True)
    plan_ref[PLACE : PLACE + 1, :] = line_of(owner_ref[...]) * GROUP + rank
    rank_down = jnp.sum(jnp.where(lane < row, ones, 0), axis=1, keepdims=True)
    wanted = jnp.zeros((1, N_SEQ), jnp.int32)
    for d in range(PLANE):
        there = (d // Y) * (Z * Y) + height_of(me) * Y + d % Y
        wanted = jnp.where((lane[:1] >> 4) == d, packing_ref[there] >> 4, wanted)
    held = ((row >> 4) == wanted) & (line_of(down) == line_of(me))
    found = held & (rank_down == (lane & 15))
    plan_ref[SOURCE : SOURCE + 1, :] = jnp.sum(
        jnp.where(found, height_of(down), 0), axis=0, keepdims=True
    )
    plan_ref[COUNT : COUNT + 1, :] = jnp.sum(held.astype(jnp.int32), axis=0, keepdims=True)
    choice = sum((most > n).astype(jnp.int32) for n in SLOT_COUNTS[:-1])
    plan_ref[CHOICE : CHOICE + 1, :] = jnp.broadcast_to(choice, (1, N_SEQ))


def make_plan(place, packing, owner):
    return pl.pallas_call(
        plan_kernel,
        out_shape=jax.ShapeDtypeStruct((4, N_SEQ), jnp.int32),
        in_specs=[SMEM, SMEM, VMEM],
        out_specs=VMEM,
    )(place, packing, owner.reshape(1, N_SEQ))


def select_kernel(slots, plan_ref, line_ref, out_ref):
    for d in range(PLANE):

        @pl.loop(0, plan_ref[COUNT, d * GROUP])
        def _(c, d=d):
            out_ref[d * slots + c] = line_ref[plan_ref[SOURCE, d * GROUP + c]]


def select(plan, line, slots):
    out = pl.pallas_call(
        functools.partial(select_kernel, slots),
        out_shape=jax.ShapeDtypeStruct((PLANE * slots, PIECE, 2 * KV_WIDTH), BF16),
        in_specs=[SMEM, VMEM],
        out_specs=VMEM,
        compiler_params=params(16),
    )(plan, line)
    return out.reshape(PLANE, slots * PIECE, 2 * KV_WIDTH)


def pack_kernel(place_ref, q_ref, g_ref, kv_ref, piece_ref, *refs):
    row_refs, line_ref, kv_here, piece_here, sems = refs[:N_HEAD], *refs[N_HEAD:]
    fetch_piece = pltpu.make_async_copy(piece_ref, piece_here, sems.at[0])
    fetch_kv = pltpu.make_async_copy(kv_ref, kv_here, sems.at[1])
    fetch_piece.start()
    fetch_kv.start()
    others = [place_ref[1] ^ k for k in range(N_HEAD)]
    fetches = []
    for k, (other, out_ref) in enumerate(zip(others, row_refs)):
        wide = pl.ds(pl.multiple_of(other * Q_WIDTH, Q_WIDTH), Q_WIDTH)
        for i, ref in enumerate((q_ref, g_ref)):
            here = out_ref.at[:, i * Q_WIDTH : (i + 1) * Q_WIDTH]
            fetches.append(pltpu.make_async_copy(ref.at[:, wide], here, sems.at[2 + 2 * k + i]))
            fetches[-1].start()
    fetch_piece.wait()
    flat = jnp.concatenate([piece_here[:, 0, :], piece_here[:, 1, :]], axis=1)
    for z in range(Z):
        line_ref[z] = flat
    fetch_kv.wait()
    for other, out_ref in zip(others, row_refs):
        narrow = pl.ds(pl.multiple_of(other * KV_WIDTH, KV_WIDTH), KV_WIDTH)
        for i in range(2):
            lo = 2 * Q_WIDTH + i * KV_WIDTH
            out_ref[:, lo : lo + KV_WIDTH] = kv_here[:, i, narrow]
    for fetch in fetches:
        fetch.wait()


def pack(place, queries, grads, kv, piece):
    return pl.pallas_call(
        pack_kernel,
        out_shape=(jax.ShapeDtypeStruct((LOCAL_ROWS, IN_WIDTH), BF16),) * N_HEAD
        + (jax.ShapeDtypeStruct((Z, PIECE, 2 * KV_WIDTH), BF16),),
        in_specs=[SMEM] + [pl.BlockSpec(memory_space=pltpu.HBM)] * 4,
        out_specs=(VMEM,) * (N_HEAD + 1),
        scratch_shapes=[
            pltpu.VMEM(kv.shape, BF16),
            pltpu.VMEM(piece.shape, BF16),
            pltpu.SemaphoreType.DMA((2 + 2 * N_HEAD,)),
        ],
        compiler_params=params(16),
    )(place, *[pltpu.with_memory_space_constraint(x, pltpu.HBM) for x in (queries, grads, kv, piece)])


def unpack_kernel(place_ref, *refs):
    q_ref, kv_ref = refs[N_HEAD:]
    for k, in_ref in enumerate(refs[N_HEAD - 1 :: -1]):
        other = place_ref[1] ^ k
        wide = pl.ds(pl.multiple_of(other * Q_WIDTH, Q_WIDTH), Q_WIDTH)
        narrow = pl.ds(pl.multiple_of(other * KV_WIDTH, KV_WIDTH), KV_WIDTH)
        q_ref[:, wide] = in_ref[:, :Q_WIDTH]
        kv_ref[:, 0, narrow] = in_ref[:, Q_WIDTH : Q_WIDTH + KV_WIDTH]
        kv_ref[:, 1, narrow] = in_ref[:, Q_WIDTH + KV_WIDTH :]


def unpack_rows(place, blocks):
    return pl.pallas_call(
        unpack_kernel,
        out_shape=(
            jax.ShapeDtypeStruct((LOCAL_ROWS, N_HEAD * Q_WIDTH), BF16),
            jax.ShapeDtypeStruct((LOCAL_ROWS, 2, N_HEAD * KV_WIDTH), BF16),
        ),
        in_specs=[SMEM] + [VMEM] * N_HEAD,
        out_specs=(VMEM, VMEM),
        compiler_params=params(16),
    )(place, *reversed(blocks))


def slots_of(place_ref, packing_ref, plan_ref, slots):
    first = (packing_ref[place_ref[0]] >> 4) << 4
    places = [plan_ref[PLACE, first + j] for j in range(GROUP)]
    return [(place >> 4) * slots + (place & 15) for place in places]


def collect_kernel(slots, place_ref, packing_ref, plan_ref, parts_ref, out_ref):
    for j, at in enumerate(slots_of(place_ref, packing_ref, plan_ref, slots)):
        out_ref[j * PIECE : (j + 1) * PIECE] = parts_ref[at]


def collect(place, packing, plan, parts, slots):
    return pl.pallas_call(
        functools.partial(collect_kernel, slots),
        out_shape=jax.ShapeDtypeStruct((PROMPT, 2 * KV_WIDTH), BF16),
        in_specs=[SMEM, SMEM, SMEM, VMEM],
        out_specs=VMEM,
        compiler_params=params(16),
    )(place, packing, plan, parts.reshape(PLANE * slots, PIECE, 2 * KV_WIDTH))


def scatter_kernel(slots, place_ref, packing_ref, plan_ref, rows_ref, out_ref):
    for j, at in enumerate(slots_of(place_ref, packing_ref, plan_ref, slots)):
        out_ref[at] = rows_ref[j * PIECE : (j + 1) * PIECE]


def scatter(place, packing, plan, rows, slots):
    out = pl.pallas_call(
        functools.partial(scatter_kernel, slots),
        out_shape=jax.ShapeDtypeStruct((PLANE * slots, PIECE, 2 * KV_WIDTH), BF16),
        in_specs=[SMEM, SMEM, SMEM, VMEM],
        out_specs=VMEM,
        compiler_params=params(16),
    )(place, packing, plan, rows)
    return out.reshape(PLANE, slots * PIECE, 2 * KV_WIDTH)


def sum_plane_kernel(slots, plan_ref, part_ref, out_ref, total_ref):
    total_ref[...] = jnp.zeros_like(total_ref)
    for d in range(PLANE):

        @pl.loop(0, plan_ref[COUNT, d * GROUP])
        def _(c, d=d):
            z = plan_ref[SOURCE, d * GROUP + c]
            total_ref[z] = total_ref[z] + part_ref[d * slots + c].astype(F32)

    out_ref[...] = total_ref[...].astype(BF16)


def sum_plane(plan, parts, slots):
    shape = (Z, PIECE, 2 * KV_WIDTH)
    return pl.pallas_call(
        functools.partial(sum_plane_kernel, slots),
        out_shape=jax.ShapeDtypeStruct(shape, BF16),
        in_specs=[SMEM, VMEM],
        out_specs=VMEM,
        scratch_shapes=[pltpu.VMEM(shape, F32)],
        compiler_params=params(16),
    )(plan, parts.reshape(PLANE * slots, PIECE, 2 * KV_WIDTH))


def sum_line_kernel(in_ref, out_ref):
    total = in_ref[0].astype(F32)
    for i in range(1, Z):
        total += in_ref[i].astype(F32)
    out_ref[:, 0, :] = total[:, :KV_WIDTH]
    out_ref[:, 1, :] = total[:, KV_WIDTH:]


def sum_line(parts):
    return pl.pallas_call(
        sum_line_kernel,
        out_shape=jax.ShapeDtypeStruct((PIECE, 2, KV_WIDTH), F32),
        in_specs=[VMEM],
        out_specs=VMEM,
        compiler_params=params(16),
    )(parts)


def slot_index(shape, dim, head, first=0):
    row = (lax.broadcasted_iota(jnp.int32, shape, dim) + first) % SLOTS
    return ((row // LOCAL_ROWS) ^ head) * LOCAL_ROWS + row % LOCAL_ROWS


def attention_kernel(place_ref, packing_ref, lengths_ref, *refs):
    row_refs, prompt_ref, refs = refs[N_HEAD - 1 :: -1], refs[N_HEAD], refs[N_HEAD + 1 :]
    back_refs, grads_ref, refs = refs[:N_HEAD], refs[N_HEAD], refs[N_HEAD + 1 :]
    key_ref, value_ref, weight_ref, dscore_ref = refs

    def rows_of(lo):
        return jnp.concatenate([ref[:, lo : lo + HEAD] for ref in row_refs], axis=0)

    def give_back(block, lo):
        for k, ref in enumerate(back_refs):
            ref[:, lo : lo + HEAD] = block[k * LOCAL_ROWS : (k + 1) * LOCAL_ROWS]

    length = lengths_ref[packing_ref[place_ref[0]]]
    key_ref[:PROMPT] = prompt_ref[:, :KV_WIDTH]
    value_ref[:PROMPT] = prompt_ref[:, KV_WIDTH:]
    for g in range(KV_LOCAL):
        cols = slice(g * HEAD, (g + 1) * HEAD)
        key_ref[PROMPT:, cols] = rows_of(2 * Q_WIDTH + g * HEAD)
        value_ref[PROMPT:, cols] = rows_of(2 * Q_WIDTH + KV_WIDTH + g * HEAD)

    width = CHUNK * SLOTS
    head = place_ref[1]
    query_pos = slot_index((1, width), 1, head)
    used = query_pos < length
    strips = [slice(lo, lo + STRIP) for lo in range(0, KEYS, STRIP)]

    def fold(x):
        return jnp.sum(x.reshape(STRIP // 8, 8, width), axis=0)

    for g in range(KV_LOCAL):
        cols = slice(g * HEAD, (g + 1) * HEAD)
        keys, values = key_ref[:, cols], value_ref[:, cols]
        keys_down = keys.T
        queries, out_grads = [], []
        for c in range(PER_GROUP // CHUNK):
            at = [(g * PER_GROUP + c * CHUNK + i) * HEAD for i in range(CHUNK)]
            query = jnp.concatenate([rows_of(lo) for lo in at], axis=0)
            out_grad = jnp.concatenate([rows_of(Q_WIDTH + lo) for lo in at], axis=0)
            queries.append(query)
            out_grads.append(out_grad)
            score = dot(keys, query, ((1,), (1,)))
            dprob = dot(values, out_grad, ((1,), (1,)))
            top = None
            scores = []
            for strip in strips:
                part = score[strip]
                if strip.start >= PROMPT:
                    key_pos = slot_index((STRIP, 1), 0, head, strip.start - PROMPT)
                    part = jnp.where(key_pos <= query_pos, part, -jnp.inf)
                scores.append(part)
                most = jnp.max(part.reshape(STRIP // 8, 8, width), axis=0)
                top = most if top is None else jnp.maximum(top, most)
            shift = jnp.max(top, axis=0, keepdims=True) * EXP2_SCALE
            raised, total, moment = [], 0.0, 0.0
            for strip, part in zip(strips, scores):
                part = jnp.exp2(part * EXP2_SCALE - shift)
                raised.append(part)
                total += fold(part)
                moment += fold(part * dprob[strip])
            total = jnp.sum(total, axis=0, keepdims=True)
            moment = jnp.sum(moment, axis=0, keepdims=True)
            scale = jnp.where(used, 1.0 / total, 0.0)
            delta = moment * scale
            here = slice(c * width, (c + 1) * width)
            for strip, part in zip(strips, raised):
                weight = part * scale
                weight_ref[strip, here] = weight.astype(BF16)
                dscore_ref[strip, here] = (weight * (dprob[strip] - delta)).astype(BF16)
            query_grad = dot(keys_down, dscore_ref[:, here], ((1,), (0,)))
            query_grad = (query_grad * INV_ROOT).astype(BF16).T
            for i, lo in enumerate(at):
                give_back(query_grad[i * SLOTS : (i + 1) * SLOTS], lo)
        key_grad = dot(dscore_ref[...], jnp.concatenate(queries, axis=0), ((1,), (0,))) * INV_ROOT
        value_grad = dot(weight_ref[...], jnp.concatenate(out_grads, axis=0), ((1,), (0,)))
        for slot, grad in enumerate((key_grad, value_grad)):
            grad = grad.astype(BF16)
            lo = slot * KV_WIDTH + g * HEAD
            grads_ref[:, lo : lo + HEAD] = grad[:PROMPT]
            give_back(grad[PROMPT:], Q_WIDTH + lo)


def attention(place, packing, lengths, rows, prompt):
    flops = 2 * 5 * KEYS * Q_WIDTH // HEAD * SLOTS * HEAD
    block = jax.ShapeDtypeStruct((LOCAL_ROWS, OUT_WIDTH), BF16)
    *back, grads = pl.pallas_call(
        attention_kernel,
        out_shape=(block,) * N_HEAD + (jax.ShapeDtypeStruct((PROMPT, 2 * KV_WIDTH), BF16),),
        in_specs=[SMEM] * 3 + [VMEM] * (N_HEAD + 1),
        out_specs=(VMEM,) * (N_HEAD + 1),
        scratch_shapes=[
            pltpu.VMEM((KEYS, KV_WIDTH), BF16),
            pltpu.VMEM((KEYS, KV_WIDTH), BF16),
            pltpu.VMEM((KEYS, PER_GROUP * SLOTS), BF16),
            pltpu.VMEM((KEYS, PER_GROUP * SLOTS), BF16),
        ],
        compiler_params=params(32),
        cost_estimate=pl.CostEstimate(
            flops=flops, bytes_accessed=6 * 2**20, transcendentals=KEYS * SLOTS * 16
        ),
    )(place, packing, lengths, *reversed(rows), prompt)
    return back, grads


def exchange(parts, axes):
    return lax.all_to_all(parts, axes, split_axis=0, concat_axis=0, tiled=True)


def swap(blocks):
    blocks = list(blocks)
    for k in reversed(range(1, N_HEAD)):
        pairs = [(i, i ^ k) for i in range(N_HEAD)]
        blocks[k] = lax.ppermute(blocks[k], ("xh", "c"), pairs)
    return blocks


def shards(queries, out_grads, response_kv, prompt_kv, packing, lengths, owner):
    place = jnp.stack([lax.axis_index(("xl", "z", "y")), lax.axis_index(("xh", "c"))])
    place = place.astype(jnp.int32)
    plane = ("xl", "y")
    *rows, line = pack(place, queries, out_grads, response_kv, prompt_kv)
    line = exchange(line, "z")
    plan = make_plan(place, packing, owner)
    rows = swap(rows)

    def gather(slots, line):
        parts = exchange(select(plan, line, slots), plane)
        return collect(place, packing, plan, parts, slots)

    def reduce(slots, grads):
        parts = exchange(scatter(place, packing, plan, grads, slots), plane)
        return sum_plane(plan, parts, slots)

    choice = plan[CHOICE, 0]
    prompt = lax.switch(
        choice, [functools.partial(gather, slots) for slots in SLOT_COUNTS], line
    )
    back, grads = attention(place, packing, lengths, rows, prompt)
    grads = lax.switch(
        choice, [functools.partial(reduce, slots) for slots in SLOT_COUNTS], grads
    )
    grads = exchange(grads, "z")
    back = swap(back)
    query_grad, resp_grad = unpack_rows(place, back)
    return query_grad, resp_grad, sum_line(grads)


def solution(mesh):
    fine = Mesh(mesh.devices.reshape(X_LO, Z, Y, 2, 2), ("xl", "z", "y", "xh", "c"))
    seq, head = ("xl", "z", "y"), ("xh", "c")
    return jax.shard_map(
        shards,
        mesh=fine,
        in_specs=(
            P(seq + head, None),
            P(seq + head, None),
            P(seq + head, None, None),
            P(seq, None, head),
            P(),
            P(),
            P(),
        ),
        out_specs=(
            P(seq + head, None),
            P(seq + head, None, None),
            P(seq, None, head),
        ),
        check_vma=False,
    )
```

```python
import functools
import math

import jax
import jax.numpy as jnp
from jax import lax
from jax.experimental import pallas as pl
from jax.experimental.pallas import tpu as pltpu
from jax.sharding import Mesh
from jax.sharding import PartitionSpec as P

QUERY_HEADS = 64
KEY_VALUE_HEADS = 8
HEAD = 128
GROUP = 16
PIECE = 16
PROMPT = GROUP * PIECE
SLOTS = 128
KEYS = PROMPT + SLOTS
X_LO, Z, Y = 2, 16, 4
PLANE = X_LO * Y
N_SEQ = PLANE * Z
SLOT_COUNTS = (4, 5, 6, 7, 8, GROUP)
N_HEAD = 4
LOCAL_ROWS = SLOTS // N_HEAD
KV_LOCAL = KEY_VALUE_HEADS // N_HEAD
PER_GROUP = QUERY_HEADS // KEY_VALUE_HEADS
Q_WIDTH = KV_LOCAL * PER_GROUP * HEAD
KV_WIDTH = KV_LOCAL * HEAD
IN_WIDTH = 2 * Q_WIDTH + 2 * KV_WIDTH
OUT_WIDTH = Q_WIDTH + 2 * KV_WIDTH
CHUNK, STRIP = 8, 64
INV_ROOT = 1.0 / math.sqrt(HEAD)
EXP2_SCALE = INV_ROOT / math.log(2.0)

BF16 = jnp.bfloat16
F32 = jnp.float32
PLACE, SOURCE, COUNT, CHOICE = range(4)

SMEM = pl.BlockSpec(memory_space=pltpu.SMEM)
VMEM = pl.BlockSpec(memory_space=pltpu.VMEM)


def params(mib):
    return pltpu.CompilerParams(vmem_limit_bytes=mib * 2**20)


def dot(a, b, contract):
    return lax.dot_general(a, b, (contract, ((), ())), preferred_element_type=F32)


def line_of(s):
    return ((s >> 6) << 2) | (s & 3)


def height_of(s):
    return (s >> 2) & 15


def plan_kernel(place_ref, packing_ref, owner_ref, plan_ref):
    me = place_ref[0]
    square = (N_SEQ, N_SEQ)
    lane = lax.broadcasted_iota(jnp.int32, square, 1)
    row = lax.broadcasted_iota(jnp.int32, square, 0)
    across = jnp.broadcast_to(owner_ref[...], square)
    down = across.T
    same = (line_of(down) == line_of(across)) & ((row >> 4) == (lane >> 4))
    ones = same.astype(jnp.int32)
    most = jnp.max(jnp.sum(ones, axis=0, keepdims=True), axis=1, keepdims=True)
    rank = jnp.sum(jnp.where(row < lane, ones, 0), axis=0, keepdims=True)
    plan_ref[PLACE : PLACE + 1, :] = line_of(owner_ref[...]) * GROUP + rank
    rank_down = jnp.sum(jnp.where(lane < row, ones, 0), axis=1, keepdims=True)
    wanted = jnp.zeros((1, N_SEQ), jnp.int32)
    for d in range(PLANE):
        there = (d // Y) * (Z * Y) + height_of(me) * Y + d % Y
        wanted = jnp.where((lane[:1] >> 4) == d, packing_ref[there] >> 4, wanted)
    held = ((row >> 4) == wanted) & (line_of(down) == line_of(me))
    found = held & (rank_down == (lane & 15))
    plan_ref[SOURCE : SOURCE + 1, :] = jnp.sum(
        jnp.where(found, height_of(down), 0), axis=0, keepdims=True
    )
    plan_ref[COUNT : COUNT + 1, :] = jnp.sum(held.astype(jnp.int32), axis=0, keepdims=True)
    choice = sum((most > n).astype(jnp.int32) for n in SLOT_COUNTS[:-1])
    plan_ref[CHOICE : CHOICE + 1, :] = jnp.broadcast_to(choice, (1, N_SEQ))


def make_plan(place, packing, owner):
    return pl.pallas_call(
        plan_kernel,
        out_shape=jax.ShapeDtypeStruct((4, N_SEQ), jnp.int32),
        in_specs=[SMEM, SMEM, VMEM],
        out_specs=VMEM,
    )(place, packing, owner.reshape(1, N_SEQ))


def select_kernel(slots, plan_ref, line_ref, out_ref):
    for d in range(PLANE):

        @pl.loop(0, plan_ref[COUNT, d * GROUP])
        def _(c, d=d):
            out_ref[d * slots + c] = line_ref[plan_ref[SOURCE, d * GROUP + c]]


def select(plan, line, slots):
    out = pl.pallas_call(
        functools.partial(select_kernel, slots),
        out_shape=jax.ShapeDtypeStruct((PLANE * slots, PIECE, 2 * KV_WIDTH), BF16),
        in_specs=[SMEM, VMEM],
        out_specs=VMEM,
        compiler_params=params(16),
    )(plan, line)
    return out.reshape(PLANE, slots * PIECE, 2 * KV_WIDTH)


def pack_kernel(q_ref, g_ref, kv_ref, piece_ref, *refs):
    row_refs, line_ref, kv_here, piece_here, line_here, sems = refs[:N_HEAD], *refs[N_HEAD:]
    fetch_piece = pltpu.make_async_copy(piece_ref, piece_here, sems.at[0])
    fetch_kv = pltpu.make_async_copy(kv_ref, kv_here, sems.at[1])
    store_line = pltpu.make_async_copy(line_here, line_ref, sems.at[2])
    fetch_piece.start()
    fetch_kv.start()
    head = lax.axis_index("xh") * 2 + lax.axis_index("c")
    others = [head ^ k for k in range(N_HEAD)]
    fetches = []
    for k in reversed(range(N_HEAD)):
        wide = pl.ds(pl.multiple_of(others[k] * Q_WIDTH, Q_WIDTH), Q_WIDTH)
        for i, ref in enumerate((q_ref, g_ref)):
            here = row_refs[k].at[:, i * Q_WIDTH : (i + 1) * Q_WIDTH]
            fetches.append(pltpu.make_async_copy(ref.at[:, wide], here, sems.at[3 + 2 * k + i]))
            fetches[-1].start()
    fetch_piece.wait()
    flat = jnp.concatenate([piece_here[:, 0, :], piece_here[:, 1, :]], axis=1)
    for z in range(Z):
        line_here[z] = flat
    store_line.start()
    fetch_kv.wait()
    for other, out_ref in zip(others, row_refs):
        narrow = pl.ds(pl.multiple_of(other * KV_WIDTH, KV_WIDTH), KV_WIDTH)
        for i in range(2):
            lo = 2 * Q_WIDTH + i * KV_WIDTH
            out_ref[:, lo : lo + KV_WIDTH] = kv_here[:, i, narrow]
    for fetch in fetches:
        fetch.wait()
    store_line.wait()


def pack(queries, grads, kv, piece):
    args = [pltpu.with_memory_space_constraint(x, pltpu.HBM) for x in (queries, grads, kv, piece)]
    line = jax.ShapeDtypeStruct((Z, PIECE, 2 * KV_WIDTH), BF16)
    hbm = pl.BlockSpec(memory_space=pltpu.HBM)
    return pl.pallas_call(
        pack_kernel,
        out_shape=(jax.ShapeDtypeStruct((LOCAL_ROWS, IN_WIDTH), BF16),) * N_HEAD + (line,),
        in_specs=[hbm] * 4,
        out_specs=(VMEM,) * N_HEAD + (hbm,),
        scratch_shapes=[
            pltpu.VMEM(kv.shape, BF16),
            pltpu.VMEM(piece.shape, BF16),
            pltpu.VMEM(line.shape, BF16),
            pltpu.SemaphoreType.DMA((3 + 2 * N_HEAD,)),
        ],
        compiler_params=params(16),
    )(*args)


def unpack_kernel(place_ref, *refs):
    q_ref, kv_ref = refs[N_HEAD:]
    for k, in_ref in enumerate(refs[N_HEAD - 1 :: -1]):
        other = place_ref[1] ^ k
        wide = pl.ds(pl.multiple_of(other * Q_WIDTH, Q_WIDTH), Q_WIDTH)
        narrow = pl.ds(pl.multiple_of(other * KV_WIDTH, KV_WIDTH), KV_WIDTH)
        q_ref[:, wide] = in_ref[:, :Q_WIDTH]
        kv_ref[:, 0, narrow] = in_ref[:, Q_WIDTH : Q_WIDTH + KV_WIDTH]
        kv_ref[:, 1, narrow] = in_ref[:, Q_WIDTH + KV_WIDTH :]


def unpack_rows(place, blocks):
    return pl.pallas_call(
        unpack_kernel,
        out_shape=(
            jax.ShapeDtypeStruct((LOCAL_ROWS, N_HEAD * Q_WIDTH), BF16),
            jax.ShapeDtypeStruct((LOCAL_ROWS, 2, N_HEAD * KV_WIDTH), BF16),
        ),
        in_specs=[SMEM] + [VMEM] * N_HEAD,
        out_specs=(VMEM, VMEM),
        compiler_params=params(16),
    )(place, *reversed(blocks))


def slots_of(place_ref, packing_ref, plan_ref, slots):
    first = (packing_ref[place_ref[0]] >> 4) << 4
    places = [plan_ref[PLACE, first + j] for j in range(GROUP)]
    return [(place >> 4) * slots + (place & 15) for place in places]


def collect_kernel(slots, place_ref, packing_ref, plan_ref, parts_ref, out_ref):
    for j, at in enumerate(slots_of(place_ref, packing_ref, plan_ref, slots)):
        out_ref[j * PIECE : (j + 1) * PIECE] = parts_ref[at]


def collect(place, packing, plan, parts, slots):
    return pl.pallas_call(
        functools.partial(collect_kernel, slots),
        out_shape=jax.ShapeDtypeStruct((PROMPT, 2 * KV_WIDTH), BF16),
        in_specs=[SMEM, SMEM, SMEM, VMEM],
        out_specs=VMEM,
        compiler_params=params(16),
    )(place, packing, plan, parts.reshape(PLANE * slots, PIECE, 2 * KV_WIDTH))


def scatter_kernel(slots, place_ref, packing_ref, plan_ref, rows_ref, out_ref):
    for j, at in enumerate(slots_of(place_ref, packing_ref, plan_ref, slots)):
        out_ref[at] = rows_ref[j * PIECE : (j + 1) * PIECE]


def scatter(place, packing, plan, rows, slots):
    out = pl.pallas_call(
        functools.partial(scatter_kernel, slots),
        out_shape=jax.ShapeDtypeStruct((PLANE * slots, PIECE, 2 * KV_WIDTH), BF16),
        in_specs=[SMEM, SMEM, SMEM, VMEM],
        out_specs=VMEM,
        compiler_params=params(16),
    )(place, packing, plan, rows)
    return out.reshape(PLANE, slots * PIECE, 2 * KV_WIDTH)


def sum_plane_kernel(slots, plan_ref, part_ref, out_ref, total_ref):
    total_ref[...] = jnp.zeros_like(total_ref)
    for d in range(PLANE):

        @pl.loop(0, plan_ref[COUNT, d * GROUP])
        def _(c, d=d):
            z = plan_ref[SOURCE, d * GROUP + c]
            total_ref[z] = total_ref[z] + part_ref[d * slots + c].astype(F32)

    out_ref[...] = total_ref[...].astype(BF16)


def sum_plane(plan, parts, slots):
    shape = (Z, PIECE, 2 * KV_WIDTH)
    return pl.pallas_call(
        functools.partial(sum_plane_kernel, slots),
        out_shape=jax.ShapeDtypeStruct(shape, BF16),
        in_specs=[SMEM, VMEM],
        out_specs=VMEM,
        scratch_shapes=[pltpu.VMEM(shape, F32)],
        compiler_params=params(16),
    )(plan, parts.reshape(PLANE * slots, PIECE, 2 * KV_WIDTH))


def sum_line_kernel(in_ref, out_ref):
    total = in_ref[0].astype(F32)
    for i in range(1, Z):
        total += in_ref[i].astype(F32)
    out_ref[:, 0, :] = total[:, :KV_WIDTH]
    out_ref[:, 1, :] = total[:, KV_WIDTH:]


def sum_line(parts):
    return pl.pallas_call(
        sum_line_kernel,
        out_shape=jax.ShapeDtypeStruct((PIECE, 2, KV_WIDTH), F32),
        in_specs=[VMEM],
        out_specs=VMEM,
        compiler_params=params(16),
    )(parts)


def slot_index(shape, dim, head, first=0):
    row = (lax.broadcasted_iota(jnp.int32, shape, dim) + first) % SLOTS
    return ((row // LOCAL_ROWS) ^ head) * LOCAL_ROWS + row % LOCAL_ROWS


def attention_kernel(place_ref, packing_ref, lengths_ref, *refs):
    row_refs, prompt_ref, refs = refs[N_HEAD - 1 :: -1], refs[N_HEAD], refs[N_HEAD + 1 :]
    back_refs, grads_ref, refs = refs[:N_HEAD], refs[N_HEAD], refs[N_HEAD + 1 :]
    key_ref, value_ref, weight_ref, dscore_ref = refs

    def rows_of(lo):
        return jnp.concatenate([ref[:, lo : lo + HEAD] for ref in row_refs], axis=0)

    def give_back(block, lo):
        for k, ref in enumerate(back_refs):
            ref[:, lo : lo + HEAD] = block[k * LOCAL_ROWS : (k + 1) * LOCAL_ROWS]

    length = lengths_ref[packing_ref[place_ref[0]]]
    key_ref[:PROMPT] = prompt_ref[:, :KV_WIDTH]
    value_ref[:PROMPT] = prompt_ref[:, KV_WIDTH:]
    for g in range(KV_LOCAL):
        cols = slice(g * HEAD, (g + 1) * HEAD)
        key_ref[PROMPT:, cols] = rows_of(2 * Q_WIDTH + g * HEAD)
        value_ref[PROMPT:, cols] = rows_of(2 * Q_WIDTH + KV_WIDTH + g * HEAD)

    width = CHUNK * SLOTS
    head = place_ref[1]
    query_pos = slot_index((1, width), 1, head)
    used = query_pos < length
    strips = [slice(lo, lo + STRIP) for lo in range(0, KEYS, STRIP)]

    def fold(x):
        return jnp.sum(x.reshape(STRIP // 8, 8, width), axis=0)

    for g in range(KV_LOCAL):
        cols = slice(g * HEAD, (g + 1) * HEAD)
        keys, values = key_ref[:, cols], value_ref[:, cols]
        keys_down = keys.T
        queries, out_grads = [], []
        for c in range(PER_GROUP // CHUNK):
            at = [(g * PER_GROUP + c * CHUNK + i) * HEAD for i in range(CHUNK)]
            query = jnp.concatenate([rows_of(lo) for lo in at], axis=0)
            out_grad = jnp.concatenate([rows_of(Q_WIDTH + lo) for lo in at], axis=0)
            queries.append(query)
            out_grads.append(out_grad)
            score = dot(keys, query, ((1,), (1,)))
            dprob = dot(values, out_grad, ((1,), (1,)))
            top = None
            scores = []
            for strip in strips:
                part = score[strip]
                if strip.start >= PROMPT:
                    key_pos = slot_index((STRIP, 1), 0, head, strip.start - PROMPT)
                    part = jnp.where(key_pos <= query_pos, part, -jnp.inf)
                scores.append(part)
                most = jnp.max(part.reshape(STRIP // 8, 8, width), axis=0)
                top = most if top is None else jnp.maximum(top, most)
            shift = jnp.max(top, axis=0, keepdims=True) * EXP2_SCALE
            raised, total, moment = [], 0.0, 0.0
            for strip, part in zip(strips, scores):
                part = jnp.exp2(part * EXP2_SCALE - shift)
                raised.append(part)
                total += fold(part)
                moment += fold(part * dprob[strip])
            total = jnp.sum(total, axis=0, keepdims=True)
            moment = jnp.sum(moment, axis=0, keepdims=True)
            scale = jnp.where(used, 1.0 / total, 0.0)
            delta = moment * scale
            here = slice(c * width, (c + 1) * width)
            for strip, part in zip(strips, raised):
                weight = part * scale
                weight_ref[strip, here] = weight.astype(BF16)
                dscore_ref[strip, here] = (weight * (dprob[strip] - delta)).astype(BF16)
            query_grad = dot(keys_down, dscore_ref[:, here], ((1,), (0,)))
            query_grad = (query_grad * INV_ROOT).astype(BF16).T
            for i, lo in enumerate(at):
                give_back(query_grad[i * SLOTS : (i + 1) * SLOTS], lo)
        key_grad = dot(dscore_ref[...], jnp.concatenate(queries, axis=0), ((1,), (0,))) * INV_ROOT
        value_grad = dot(weight_ref[...], jnp.concatenate(out_grads, axis=0), ((1,), (0,)))
        for slot, grad in enumerate((key_grad, value_grad)):
            grad = grad.astype(BF16)
            lo = slot * KV_WIDTH + g * HEAD
            grads_ref[:, lo : lo + HEAD] = grad[:PROMPT]
            give_back(grad[PROMPT:], Q_WIDTH + lo)


def attention(place, packing, lengths, rows, prompt):
    flops = 2 * 5 * KEYS * Q_WIDTH // HEAD * SLOTS * HEAD
    block = jax.ShapeDtypeStruct((LOCAL_ROWS, OUT_WIDTH), BF16)
    *back, grads = pl.pallas_call(
        attention_kernel,
        out_shape=(block,) * N_HEAD + (jax.ShapeDtypeStruct((PROMPT, 2 * KV_WIDTH), BF16),),
        in_specs=[SMEM] * 3 + [VMEM] * (N_HEAD + 1),
        out_specs=(VMEM,) * (N_HEAD + 1),
        scratch_shapes=[
            pltpu.VMEM((KEYS, KV_WIDTH), BF16),
            pltpu.VMEM((KEYS, KV_WIDTH), BF16),
            pltpu.VMEM((KEYS, PER_GROUP * SLOTS), BF16),
            pltpu.VMEM((KEYS, PER_GROUP * SLOTS), BF16),
        ],
        compiler_params=params(32),
        cost_estimate=pl.CostEstimate(
            flops=flops, bytes_accessed=6 * 2**20, transcendentals=KEYS * SLOTS * 16
        ),
    )(place, packing, lengths, *reversed(rows), prompt)
    return back, grads


def exchange(parts, axes):
    return lax.all_to_all(parts, axes, split_axis=0, concat_axis=0, tiled=True)


def swap(blocks):
    blocks = list(blocks)
    for k in reversed(range(1, N_HEAD)):
        pairs = [(i, i ^ k) for i in range(N_HEAD)]
        blocks[k] = lax.ppermute(blocks[k], ("xh", "c"), pairs)
    return blocks


def shards(queries, out_grads, response_kv, prompt_kv, packing, lengths, owner):
    place = jnp.stack([lax.axis_index(("xl", "z", "y")), lax.axis_index(("xh", "c"))])
    place = place.astype(jnp.int32)
    plane = ("xl", "y")
    *rows, line = pack(queries, out_grads, response_kv, prompt_kv)
    line = exchange(line, "z")
    plan = make_plan(place, packing, owner)
    rows = swap(rows)

    def gather(slots, line):
        parts = exchange(select(plan, line, slots), plane)
        return collect(place, packing, plan, parts, slots)

    def reduce(slots, grads):
        parts = exchange(scatter(place, packing, plan, grads, slots), plane)
        return sum_plane(plan, parts, slots)

    choice = plan[CHOICE, 0]
    prompt = lax.switch(
        choice, [functools.partial(gather, slots) for slots in SLOT_COUNTS], line
    )
    back, grads = attention(place, packing, lengths, rows, prompt)
    grads = lax.switch(
        choice, [functools.partial(reduce, slots) for slots in SLOT_COUNTS], grads
    )
    grads = exchange(grads, "z")
    back = swap(back)
    query_grad, resp_grad = unpack_rows(place, back)
    return query_grad, resp_grad, sum_line(grads)


def solution(mesh):
    fine = Mesh(mesh.devices.reshape(X_LO, Z, Y, 2, 2), ("xl", "z", "y", "xh", "c"))
    seq, head = ("xl", "z", "y"), ("xh", "c")
    return jax.shard_map(
        shards,
        mesh=fine,
        in_specs=(
            P(seq + head, None),
            P(seq + head, None),
            P(seq + head, None, None),
            P(seq, None, head),
            P(),
            P(),
            P(),
        ),
        out_specs=(
            P(seq + head, None),
            P(seq + head, None, None),
            P(seq, None, head),
        ),
        check_vma=False,
    )
```

```python
import functools
import math

import jax
import jax.numpy as jnp
from jax import lax
from jax.experimental import pallas as pl
from jax.experimental.pallas import tpu as pltpu
from jax.sharding import Mesh
from jax.sharding import PartitionSpec as P

QUERY_HEADS = 64
KEY_VALUE_HEADS = 8
HEAD = 128
GROUP = 16
PIECE = 16
PROMPT = GROUP * PIECE
SLOTS = 128
KEYS = PROMPT + SLOTS
X_LO, Z, Y = 2, 16, 4
PLANE = X_LO * Y
N_SEQ = PLANE * Z
SLOT_COUNTS = (4, 5, 6, 7, 8, GROUP)
N_HEAD = 4
LOCAL_ROWS = SLOTS // N_HEAD
KV_LOCAL = KEY_VALUE_HEADS // N_HEAD
PER_GROUP = QUERY_HEADS // KEY_VALUE_HEADS
Q_WIDTH = KV_LOCAL * PER_GROUP * HEAD
KV_WIDTH = KV_LOCAL * HEAD
IN_WIDTH = 2 * Q_WIDTH + 2 * KV_WIDTH
OUT_WIDTH = Q_WIDTH + 2 * KV_WIDTH
CHUNK, STRIP, AHEAD, BEHIND = 8, 64, 1, 0
INV_ROOT = 1.0 / math.sqrt(HEAD)
EXP2_SCALE = INV_ROOT / math.log(2.0)

BF16 = jnp.bfloat16
F32 = jnp.float32
PLACE, SOURCE, COUNT, CHOICE = range(4)

SMEM = pl.BlockSpec(memory_space=pltpu.SMEM)
VMEM = pl.BlockSpec(memory_space=pltpu.VMEM)


def params(mib):
    return pltpu.CompilerParams(vmem_limit_bytes=mib * 2**20)


def dot(a, b, contract):
    return lax.dot_general(a, b, (contract, ((), ())), preferred_element_type=F32)


def line_of(s):
    return ((s >> 6) << 2) | (s & 3)


def height_of(s):
    return (s >> 2) & 15


def plan_kernel(place_ref, packing_ref, owner_ref, plan_ref):
    me = place_ref[0]
    square = (N_SEQ, N_SEQ)
    lane = lax.broadcasted_iota(jnp.int32, square, 1)
    row = lax.broadcasted_iota(jnp.int32, square, 0)
    across = jnp.broadcast_to(owner_ref[...], square)
    down = across.T
    same = (line_of(down) == line_of(across)) & ((row >> 4) == (lane >> 4))
    ones = same.astype(jnp.int32)
    most = jnp.max(jnp.sum(ones, axis=0, keepdims=True), axis=1, keepdims=True)
    rank = jnp.sum(jnp.where(row < lane, ones, 0), axis=0, keepdims=True)
    plan_ref[PLACE : PLACE + 1, :] = line_of(owner_ref[...]) * GROUP + rank
    rank_down = jnp.sum(jnp.where(lane < row, ones, 0), axis=1, keepdims=True)
    wanted = jnp.zeros((1, N_SEQ), jnp.int32)
    for d in range(PLANE):
        there = (d // Y) * (Z * Y) + height_of(me) * Y + d % Y
        wanted = jnp.where((lane[:1] >> 4) == d, packing_ref[there] >> 4, wanted)
    held = ((row >> 4) == wanted) & (line_of(down) == line_of(me))
    found = held & (rank_down == (lane & 15))
    plan_ref[SOURCE : SOURCE + 1, :] = jnp.sum(
        jnp.where(found, height_of(down), 0), axis=0, keepdims=True
    )
    plan_ref[COUNT : COUNT + 1, :] = jnp.sum(held.astype(jnp.int32), axis=0, keepdims=True)
    choice = sum((most > n).astype(jnp.int32) for n in SLOT_COUNTS[:-1])
    plan_ref[CHOICE : CHOICE + 1, :] = jnp.broadcast_to(choice, (1, N_SEQ))


def make_plan(place, packing, owner):
    return pl.pallas_call(
        plan_kernel,
        out_shape=jax.ShapeDtypeStruct((4, N_SEQ), jnp.int32),
        in_specs=[SMEM, SMEM, VMEM],
        out_specs=VMEM,
    )(place, packing, owner.reshape(1, N_SEQ))


def select_kernel(slots, plan_ref, line_ref, out_ref):
    for d in range(PLANE):

        @pl.loop(0, plan_ref[COUNT, d * GROUP])
        def _(c, d=d):
            out_ref[d * slots + c] = line_ref[plan_ref[SOURCE, d * GROUP + c]]


def select(plan, line, slots):
    out = pl.pallas_call(
        functools.partial(select_kernel, slots),
        out_shape=jax.ShapeDtypeStruct((PLANE * slots, PIECE, 2 * KV_WIDTH), BF16),
        in_specs=[SMEM, VMEM],
        out_specs=VMEM,
        compiler_params=params(16),
    )(plan, line)
    return out.reshape(PLANE, slots * PIECE, 2 * KV_WIDTH)


def pack_kernel(q_ref, g_ref, kv_ref, piece_ref, *refs):
    row_refs, line_ref, kv_here, piece_here, line_here, sems = refs[:N_HEAD], *refs[N_HEAD:]
    fetch_piece = pltpu.make_async_copy(piece_ref, piece_here, sems.at[0])
    fetch_kv = pltpu.make_async_copy(kv_ref, kv_here, sems.at[1])
    store_line = pltpu.make_async_copy(line_here, line_ref, sems.at[2])
    fetch_piece.start()
    fetch_kv.start()
    head = lax.axis_index("xh") * 2 + lax.axis_index("c")
    others = [head ^ k for k in range(N_HEAD)]
    fetches = []
    for k in reversed(range(N_HEAD)):
        wide = pl.ds(pl.multiple_of(others[k] * Q_WIDTH, Q_WIDTH), Q_WIDTH)
        for i, ref in enumerate((q_ref, g_ref)):
            here = row_refs[k].at[:, i * Q_WIDTH : (i + 1) * Q_WIDTH]
            fetches.append(pltpu.make_async_copy(ref.at[:, wide], here, sems.at[3 + 2 * k + i]))
            fetches[-1].start()
    fetch_piece.wait()
    flat = jnp.concatenate([piece_here[:, 0, :], piece_here[:, 1, :]], axis=1)
    for z in range(Z):
        line_here[z] = flat
    store_line.start()
    fetch_kv.wait()
    for other, out_ref in zip(others, row_refs):
        narrow = pl.ds(pl.multiple_of(other * KV_WIDTH, KV_WIDTH), KV_WIDTH)
        for i in range(2):
            lo = 2 * Q_WIDTH + i * KV_WIDTH
            out_ref[:, lo : lo + KV_WIDTH] = kv_here[:, i, narrow]
    for fetch in fetches:
        fetch.wait()
    store_line.wait()


def pack(queries, grads, kv, piece):
    args = [pltpu.with_memory_space_constraint(x, pltpu.HBM) for x in (queries, grads, kv, piece)]
    line = jax.ShapeDtypeStruct((Z, PIECE, 2 * KV_WIDTH), BF16)
    hbm = pl.BlockSpec(memory_space=pltpu.HBM)
    return pl.pallas_call(
        pack_kernel,
        out_shape=(jax.ShapeDtypeStruct((LOCAL_ROWS, IN_WIDTH), BF16),) * N_HEAD + (line,),
        in_specs=[hbm] * 4,
        out_specs=(VMEM,) * N_HEAD + (hbm,),
        scratch_shapes=[
            pltpu.VMEM(kv.shape, BF16),
            pltpu.VMEM(piece.shape, BF16),
            pltpu.VMEM(line.shape, BF16),
            pltpu.SemaphoreType.DMA((3 + 2 * N_HEAD,)),
        ],
        compiler_params=params(16),
    )(*args)


def unpack_kernel(place_ref, *refs):
    q_ref, kv_ref = refs[N_HEAD:]
    for k, in_ref in enumerate(refs[N_HEAD - 1 :: -1]):
        other = place_ref[1] ^ k
        wide = pl.ds(pl.multiple_of(other * Q_WIDTH, Q_WIDTH), Q_WIDTH)
        narrow = pl.ds(pl.multiple_of(other * KV_WIDTH, KV_WIDTH), KV_WIDTH)
        q_ref[:, wide] = in_ref[:, :Q_WIDTH]
        kv_ref[:, 0, narrow] = in_ref[:, Q_WIDTH : Q_WIDTH + KV_WIDTH]
        kv_ref[:, 1, narrow] = in_ref[:, Q_WIDTH + KV_WIDTH :]


def unpack_rows(place, blocks):
    return pl.pallas_call(
        unpack_kernel,
        out_shape=(
            jax.ShapeDtypeStruct((LOCAL_ROWS, N_HEAD * Q_WIDTH), BF16),
            jax.ShapeDtypeStruct((LOCAL_ROWS, 2, N_HEAD * KV_WIDTH), BF16),
        ),
        in_specs=[SMEM] + [VMEM] * N_HEAD,
        out_specs=(VMEM, VMEM),
        compiler_params=params(16),
    )(place, *reversed(blocks))


def slots_of(place_ref, packing_ref, plan_ref, slots):
    first = (packing_ref[place_ref[0]] >> 4) << 4
    places = [plan_ref[PLACE, first + j] for j in range(GROUP)]
    return [(place >> 4) * slots + (place & 15) for place in places]


def collect_kernel(slots, place_ref, packing_ref, plan_ref, parts_ref, out_ref):
    for j, at in enumerate(slots_of(place_ref, packing_ref, plan_ref, slots)):
        out_ref[j * PIECE : (j + 1) * PIECE] = parts_ref[at]


def collect(place, packing, plan, parts, slots):
    return pl.pallas_call(
        functools.partial(collect_kernel, slots),
        out_shape=jax.ShapeDtypeStruct((PROMPT, 2 * KV_WIDTH), BF16),
        in_specs=[SMEM, SMEM, SMEM, VMEM],
        out_specs=VMEM,
        compiler_params=params(16),
    )(place, packing, plan, parts.reshape(PLANE * slots, PIECE, 2 * KV_WIDTH))


def sum_plane_kernel(slots, plan_ref, part_ref, out_ref, total_ref):
    total_ref[...] = jnp.zeros_like(total_ref)
    for d in range(PLANE):

        @pl.loop(0, plan_ref[COUNT, d * GROUP])
        def _(c, d=d):
            z = plan_ref[SOURCE, d * GROUP + c]
            total_ref[z] = total_ref[z] + part_ref[d * slots + c].astype(F32)

    out_ref[...] = total_ref[...].astype(BF16)


def sum_plane(plan, parts, slots):
    shape = (Z, PIECE, 2 * KV_WIDTH)
    return pl.pallas_call(
        functools.partial(sum_plane_kernel, slots),
        out_shape=jax.ShapeDtypeStruct(shape, BF16),
        in_specs=[SMEM, VMEM],
        out_specs=VMEM,
        scratch_shapes=[pltpu.VMEM(shape, F32)],
        compiler_params=params(16),
    )(plan, parts.reshape(PLANE * slots, PIECE, 2 * KV_WIDTH))


def sum_line_kernel(in_ref, out_ref):
    total = in_ref[0].astype(F32)
    for i in range(1, Z):
        total += in_ref[i].astype(F32)
    out_ref[:, 0, :] = total[:, :KV_WIDTH]
    out_ref[:, 1, :] = total[:, KV_WIDTH:]


def sum_line(parts):
    return pl.pallas_call(
        sum_line_kernel,
        out_shape=jax.ShapeDtypeStruct((PIECE, 2, KV_WIDTH), F32),
        in_specs=[VMEM],
        out_specs=VMEM,
        compiler_params=params(16),
    )(parts)


def slot_index(shape, dim, head, first=0):
    row = (lax.broadcasted_iota(jnp.int32, shape, dim) + first) % SLOTS
    return ((row // LOCAL_ROWS) ^ head) * LOCAL_ROWS + row % LOCAL_ROWS


def attention_kernel(slots, place_ref, packing_ref, lengths_ref, plan_ref, *refs):
    row_refs, prompt_ref, refs = refs[N_HEAD - 1 :: -1], refs[N_HEAD], refs[N_HEAD + 1 :]
    back_refs, grads_ref, refs = refs[:N_HEAD], refs[N_HEAD], refs[N_HEAD + 1 :]
    key_ref, value_ref, weight_ref, dscore_ref = refs

    def rows_of(lo):
        return jnp.concatenate([ref[:, lo : lo + HEAD] for ref in row_refs], axis=0)

    def give_back(block, lo):
        for k, ref in enumerate(back_refs):
            ref[:, lo : lo + HEAD] = block[k * LOCAL_ROWS : (k + 1) * LOCAL_ROWS]

    length = lengths_ref[packing_ref[place_ref[0]]]
    places = slots_of(place_ref, packing_ref, plan_ref, slots)
    key_ref[:PROMPT] = prompt_ref[:, :KV_WIDTH]
    value_ref[:PROMPT] = prompt_ref[:, KV_WIDTH:]
    for g in range(KV_LOCAL):
        cols = slice(g * HEAD, (g + 1) * HEAD)
        key_ref[PROMPT:, cols] = rows_of(2 * Q_WIDTH + g * HEAD)
        value_ref[PROMPT:, cols] = rows_of(2 * Q_WIDTH + KV_WIDTH + g * HEAD)

    width = CHUNK * SLOTS
    head = place_ref[1]
    query_pos = slot_index((1, width), 1, head)
    used = query_pos < length
    strips = [slice(lo, lo + STRIP) for lo in range(0, KEYS, STRIP)]

    def fold(x):
        return jnp.sum(x.reshape(STRIP // 8, 8, width), axis=0)

    def products(g, c):
        cols = slice(g * HEAD, (g + 1) * HEAD)
        at = [(g * PER_GROUP + c * CHUNK + i) * HEAD for i in range(CHUNK)]
        query = jnp.concatenate([rows_of(lo) for lo in at], axis=0)
        out_grad = jnp.concatenate([rows_of(Q_WIDTH + lo) for lo in at], axis=0)
        score = dot(key_ref[:, cols], query, ((1,), (1,)))
        dprob = dot(value_ref[:, cols], out_grad, ((1,), (1,)))
        return query, out_grad, score, dprob

    def softmax(g, c, score, dprob):
        top, scores = None, []
        for strip in strips:
            part = score[strip]
            if strip.start >= PROMPT:
                key_pos = slot_index((STRIP, 1), 0, head, strip.start - PROMPT)
                part = jnp.where(key_pos <= query_pos, part, -jnp.inf)
            scores.append(part)
            most = jnp.max(part.reshape(STRIP // 8, 8, width), axis=0)
            top = most if top is None else jnp.maximum(top, most)
        shift = jnp.max(top, axis=0, keepdims=True) * EXP2_SCALE
        raised, total, moment = [], 0.0, 0.0
        for strip, part in zip(strips, scores):
            part = jnp.exp2(part * EXP2_SCALE - shift)
            raised.append(part)
            total += fold(part)
            moment += fold(part * dprob[strip])
        total = jnp.sum(total, axis=0, keepdims=True)
        moment = jnp.sum(moment, axis=0, keepdims=True)
        scale = jnp.where(used, 1.0 / total, 0.0)
        delta = moment * scale
        here = slice(c * width, (c + 1) * width)
        for strip, part in zip(strips, raised):
            weight = part * scale
            weight_ref[g, strip, here] = weight.astype(BF16)
            dscore_ref[g, strip, here] = (weight * (dprob[strip] - delta)).astype(BF16)

    def query_side(g, c):
        keys_down = key_ref[:, g * HEAD : (g + 1) * HEAD].T
        grad = dot(keys_down, dscore_ref[g, :, c * width : (c + 1) * width], ((1,), (0,)))
        grad = (grad * INV_ROOT).astype(BF16).T
        for i in range(CHUNK):
            give_back(grad[i * SLOTS : (i + 1) * SLOTS], (g * PER_GROUP + c * CHUNK + i) * HEAD)

    def key_side(g, queries, out_grads):
        key_grad = dot(dscore_ref[g], jnp.concatenate(queries, axis=0), ((1,), (0,))) * INV_ROOT
        value_grad = dot(weight_ref[g], jnp.concatenate(out_grads, axis=0), ((1,), (0,)))
        for slot, grad in enumerate((key_grad, value_grad)):
            grad = grad.astype(BF16)
            lo = slot * KV_WIDTH + g * HEAD
            for j, at in enumerate(places):
                grads_ref[at, :, lo : lo + HEAD] = grad[j * PIECE : (j + 1) * PIECE]
            give_back(grad[PROMPT:], Q_WIDTH + lo)

    chunks = [(g, c) for g in range(KV_LOCAL) for c in range(PER_GROUP // CHUNK)]
    ready = {}

    def after(g, c):
        query_side(g, c)
        if c == PER_GROUP // CHUNK - 1:
            done = [ready[g, i] for i in range(c + 1)]
            key_side(g, [x[0] for x in done], [x[1] for x in done])

    for n in range(min(AHEAD, len(chunks))):
        ready[chunks[n]] = products(*chunks[n])
    for n, chunk in enumerate(chunks):
        if n + AHEAD < len(chunks):
            ready[chunks[n + AHEAD]] = products(*chunks[n + AHEAD])
        if AHEAD == 0:
            ready[chunk] = products(*chunk)
        softmax(*chunk, *ready[chunk][2:])
        if n >= BEHIND:
            after(*chunks[n - BEHIND])
    for chunk in chunks[len(chunks) - BEHIND :]:
        after(*chunk)


def attention(place, packing, lengths, plan, rows, prompt, slots):
    flops = 2 * 5 * KEYS * Q_WIDTH // HEAD * SLOTS * HEAD
    block = jax.ShapeDtypeStruct((LOCAL_ROWS, OUT_WIDTH), BF16)
    *back, grads = pl.pallas_call(
        functools.partial(attention_kernel, slots),
        out_shape=(block,) * N_HEAD
        + (jax.ShapeDtypeStruct((PLANE * slots, PIECE, 2 * KV_WIDTH), BF16),),
        in_specs=[SMEM] * 4 + [VMEM] * (N_HEAD + 1),
        out_specs=(VMEM,) * (N_HEAD + 1),
        scratch_shapes=[
            pltpu.VMEM((KEYS, KV_WIDTH), BF16),
            pltpu.VMEM((KEYS, KV_WIDTH), BF16),
            pltpu.VMEM((KV_LOCAL, KEYS, PER_GROUP * SLOTS), BF16),
            pltpu.VMEM((KV_LOCAL, KEYS, PER_GROUP * SLOTS), BF16),
        ],
        compiler_params=params(32),
        cost_estimate=pl.CostEstimate(
            flops=flops, bytes_accessed=6 * 2**20, transcendentals=KEYS * SLOTS * 16
        ),
    )(place, packing, lengths, plan, *reversed(rows), prompt)
    return back, grads.reshape(PLANE, slots * PIECE, 2 * KV_WIDTH)


def exchange(parts, axes):
    return lax.all_to_all(parts, axes, split_axis=0, concat_axis=0, tiled=True)


def swap(blocks):
    blocks = list(blocks)
    for k in reversed(range(1, N_HEAD)):
        pairs = [(i, i ^ k) for i in range(N_HEAD)]
        blocks[k] = lax.ppermute(blocks[k], ("xh", "c"), pairs)
    return blocks


def shards(queries, out_grads, response_kv, prompt_kv, packing, lengths, owner):
    place = jnp.stack([lax.axis_index(("xl", "z", "y")), lax.axis_index(("xh", "c"))])
    place = place.astype(jnp.int32)
    plane = ("xl", "y")
    *rows, line = pack(queries, out_grads, response_kv, prompt_kv)
    line = exchange(line, "z")
    plan = make_plan(place, packing, owner)
    rows = swap(rows)

    def gather(slots, line):
        parts = exchange(select(plan, line, slots), plane)
        return collect(place, packing, plan, parts, slots)

    def reduce(slots, prompt, *rows):
        back, grads = attention(place, packing, lengths, plan, rows, prompt, slots)
        return back, sum_plane(plan, exchange(grads, plane), slots)

    choice = plan[CHOICE, 0]
    prompt = lax.switch(
        choice, [functools.partial(gather, slots) for slots in SLOT_COUNTS], line
    )
    back, grads = lax.switch(
        choice, [functools.partial(reduce, slots) for slots in SLOT_COUNTS], prompt, *rows
    )
    grads = exchange(grads, "z")
    back = swap(back)
    query_grad, resp_grad = unpack_rows(place, back)
    return query_grad, resp_grad, sum_line(grads)


def solution(mesh):
    fine = Mesh(mesh.devices.reshape(X_LO, Z, Y, 2, 2), ("xl", "z", "y", "xh", "c"))
    seq, head = ("xl", "z", "y"), ("xh", "c")
    return jax.shard_map(
        shards,
        mesh=fine,
        in_specs=(
            P(seq + head, None),
            P(seq + head, None),
            P(seq + head, None, None),
            P(seq, None, head),
            P(),
            P(),
            P(),
        ),
        out_specs=(
            P(seq + head, None),
            P(seq + head, None, None),
            P(seq, None, head),
        ),
        check_vma=False,
    )
```

```python
import functools
import math

import jax
import jax.numpy as jnp
from jax import lax
from jax.experimental import pallas as pl
from jax.experimental.pallas import tpu as pltpu
from jax.sharding import Mesh
from jax.sharding import PartitionSpec as P

QUERY_HEADS = 64
KEY_VALUE_HEADS = 8
HEAD = 128
GROUP = 16
PIECE = 16
PROMPT = GROUP * PIECE
SLOTS = 128
KEYS = PROMPT + SLOTS
X_LO, Z, Y = 2, 16, 4
PLANE = X_LO * Y
N_SEQ = PLANE * Z
SLOT_COUNTS = (4, 5, 6, 7, 8, GROUP)
N_HEAD = 4
LOCAL_ROWS = SLOTS // N_HEAD
KV_LOCAL = KEY_VALUE_HEADS // N_HEAD
PER_GROUP = QUERY_HEADS // KEY_VALUE_HEADS
Q_WIDTH = KV_LOCAL * PER_GROUP * HEAD
KV_WIDTH = KV_LOCAL * HEAD
IN_WIDTH = 2 * Q_WIDTH + 2 * KV_WIDTH
OUT_WIDTH = Q_WIDTH + 2 * KV_WIDTH
CHUNK, STRIP, AHEAD, BEHIND = 8, 64, 1, 0
INV_ROOT = 1.0 / math.sqrt(HEAD)
EXP2_SCALE = INV_ROOT / math.log(2.0)

BF16 = jnp.bfloat16
F32 = jnp.float32
PLACE, SOURCE, COUNT, CHOICE = range(4)

SMEM = pl.BlockSpec(memory_space=pltpu.SMEM)
VMEM = pl.BlockSpec(memory_space=pltpu.VMEM)


def params(mib):
    return pltpu.CompilerParams(vmem_limit_bytes=mib * 2**20)


def dot(a, b, contract):
    return lax.dot_general(a, b, (contract, ((), ())), preferred_element_type=F32)


def line_of(s):
    return ((s >> 6) << 2) | (s & 3)


def height_of(s):
    return (s >> 2) & 15


def plan_kernel(place_ref, packing_ref, owner_ref, plan_ref):
    me = place_ref[0]
    square = (N_SEQ, N_SEQ)
    lane = lax.broadcasted_iota(jnp.int32, square, 1)
    row = lax.broadcasted_iota(jnp.int32, square, 0)
    across = jnp.broadcast_to(owner_ref[...], square)
    down = across.T
    same = (line_of(down) == line_of(across)) & ((row >> 4) == (lane >> 4))
    ones = same.astype(jnp.int32)
    most = jnp.max(jnp.sum(ones, axis=0, keepdims=True), axis=1, keepdims=True)
    rank = jnp.sum(jnp.where(row < lane, ones, 0), axis=0, keepdims=True)
    plan_ref[PLACE : PLACE + 1, :] = line_of(owner_ref[...]) * GROUP + rank
    rank_down = jnp.sum(jnp.where(lane < row, ones, 0), axis=1, keepdims=True)
    wanted = jnp.zeros((1, N_SEQ), jnp.int32)
    for d in range(PLANE):
        there = (d // Y) * (Z * Y) + height_of(me) * Y + d % Y
        wanted = jnp.where((lane[:1] >> 4) == d, packing_ref[there] >> 4, wanted)
    held = ((row >> 4) == wanted) & (line_of(down) == line_of(me))
    found = held & (rank_down == (lane & 15))
    plan_ref[SOURCE : SOURCE + 1, :] = jnp.sum(
        jnp.where(found, height_of(down), 0), axis=0, keepdims=True
    )
    plan_ref[COUNT : COUNT + 1, :] = jnp.sum(held.astype(jnp.int32), axis=0, keepdims=True)
    choice = sum((most > n).astype(jnp.int32) for n in SLOT_COUNTS[:-1])
    plan_ref[CHOICE : CHOICE + 1, :] = jnp.broadcast_to(choice, (1, N_SEQ))


def make_plan(place, packing, owner):
    return pl.pallas_call(
        plan_kernel,
        out_shape=jax.ShapeDtypeStruct((4, N_SEQ), jnp.int32),
        in_specs=[SMEM, SMEM, VMEM],
        out_specs=VMEM,
    )(place, packing, owner.reshape(1, N_SEQ))


def select_kernel(slots, plan_ref, line_ref, out_ref):
    for d in range(PLANE):
        for c in range(slots):
            out_ref[d * slots + c] = line_ref[plan_ref[SOURCE, d * GROUP + c]]


def select(plan, line, slots):
    out = pl.pallas_call(
        functools.partial(select_kernel, slots),
        out_shape=jax.ShapeDtypeStruct((PLANE * slots, PIECE, 2 * KV_WIDTH), BF16),
        in_specs=[SMEM, VMEM],
        out_specs=VMEM,
        compiler_params=params(16),
    )(plan, line)
    return out.reshape(PLANE, slots * PIECE, 2 * KV_WIDTH)


def pack_kernel(q_ref, g_ref, kv_ref, piece_ref, *refs):
    row_refs, line_ref, kv_here, piece_here, line_here, sems = refs[:N_HEAD], *refs[N_HEAD:]
    fetch_piece = pltpu.make_async_copy(piece_ref, piece_here, sems.at[0])
    fetch_kv = pltpu.make_async_copy(kv_ref, kv_here, sems.at[1])
    store_line = pltpu.make_async_copy(line_here, line_ref, sems.at[2])
    fetch_piece.start()
    fetch_kv.start()
    head = lax.axis_index("xh") * 2 + lax.axis_index("c")
    others = [head ^ k for k in range(N_HEAD)]
    fetches = []
    for k in reversed(range(N_HEAD)):
        wide = pl.ds(pl.multiple_of(others[k] * Q_WIDTH, Q_WIDTH), Q_WIDTH)
        for i, ref in enumerate((q_ref, g_ref)):
            here = row_refs[k].at[:, i * Q_WIDTH : (i + 1) * Q_WIDTH]
            fetches.append(pltpu.make_async_copy(ref.at[:, wide], here, sems.at[3 + 2 * k + i]))
            fetches[-1].start()
    fetch_piece.wait()
    flat = jnp.concatenate([piece_here[:, 0, :], piece_here[:, 1, :]], axis=1)
    for z in range(Z):
        line_here[z] = flat
    store_line.start()
    fetch_kv.wait()
    for other, out_ref in zip(others, row_refs):
        narrow = pl.ds(pl.multiple_of(other * KV_WIDTH, KV_WIDTH), KV_WIDTH)
        for i in range(2):
            lo = 2 * Q_WIDTH + i * KV_WIDTH
            out_ref[:, lo : lo + KV_WIDTH] = kv_here[:, i, narrow]
    for fetch in fetches:
        fetch.wait()
    store_line.wait()


def pack(queries, grads, kv, piece):
    args = [pltpu.with_memory_space_constraint(x, pltpu.HBM) for x in (queries, grads, kv, piece)]
    line = jax.ShapeDtypeStruct((Z, PIECE, 2 * KV_WIDTH), BF16)
    hbm = pl.BlockSpec(memory_space=pltpu.HBM)
    return pl.pallas_call(
        pack_kernel,
        out_shape=(jax.ShapeDtypeStruct((LOCAL_ROWS, IN_WIDTH), BF16),) * N_HEAD + (line,),
        in_specs=[hbm] * 4,
        out_specs=(VMEM,) * N_HEAD + (hbm,),
        scratch_shapes=[
            pltpu.VMEM(kv.shape, BF16),
            pltpu.VMEM(piece.shape, BF16),
            pltpu.VMEM(line.shape, BF16),
            pltpu.SemaphoreType.DMA((3 + 2 * N_HEAD,)),
        ],
        compiler_params=params(16),
    )(*args)


def unpack_kernel(place_ref, *refs):
    q_ref, kv_ref = refs[N_HEAD:]
    for k, in_ref in enumerate(refs[N_HEAD - 1 :: -1]):
        other = place_ref[1] ^ k
        wide = pl.ds(pl.multiple_of(other * Q_WIDTH, Q_WIDTH), Q_WIDTH)
        narrow = pl.ds(pl.multiple_of(other * KV_WIDTH, KV_WIDTH), KV_WIDTH)
        q_ref[:, wide] = in_ref[:, :Q_WIDTH]
        kv_ref[:, 0, narrow] = in_ref[:, Q_WIDTH : Q_WIDTH + KV_WIDTH]
        kv_ref[:, 1, narrow] = in_ref[:, Q_WIDTH + KV_WIDTH :]


def unpack_rows(place, blocks):
    return pl.pallas_call(
        unpack_kernel,
        out_shape=(
            jax.ShapeDtypeStruct((LOCAL_ROWS, N_HEAD * Q_WIDTH), BF16),
            jax.ShapeDtypeStruct((LOCAL_ROWS, 2, N_HEAD * KV_WIDTH), BF16),
        ),
        in_specs=[SMEM] + [VMEM] * N_HEAD,
        out_specs=(VMEM, VMEM),
        compiler_params=params(16),
    )(place, *reversed(blocks))


def slots_of(place_ref, packing_ref, plan_ref, slots):
    first = (packing_ref[place_ref[0]] >> 4) << 4
    places = [plan_ref[PLACE, first + j] for j in range(GROUP)]
    return [(place >> 4) * slots + (place & 15) for place in places]


def collect_kernel(slots, place_ref, packing_ref, plan_ref, parts_ref, out_ref):
    for j, at in enumerate(slots_of(place_ref, packing_ref, plan_ref, slots)):
        out_ref[j * PIECE : (j + 1) * PIECE] = parts_ref[at]


def collect(place, packing, plan, parts, slots):
    return pl.pallas_call(
        functools.partial(collect_kernel, slots),
        out_shape=jax.ShapeDtypeStruct((PROMPT, 2 * KV_WIDTH), BF16),
        in_specs=[SMEM, SMEM, SMEM, VMEM],
        out_specs=VMEM,
        compiler_params=params(16),
    )(place, packing, plan, parts.reshape(PLANE * slots, PIECE, 2 * KV_WIDTH))


def sum_plane_kernel(slots, plan_ref, part_ref, out_ref, total_ref):
    total_ref[...] = jnp.zeros_like(total_ref)
    for d in range(PLANE):

        @pl.loop(0, plan_ref[COUNT, d * GROUP])
        def _(c, d=d):
            z = plan_ref[SOURCE, d * GROUP + c]
            total_ref[z] = total_ref[z] + part_ref[d * slots + c].astype(F32)

    out_ref[...] = total_ref[...].astype(BF16)


def sum_plane(plan, parts, slots):
    shape = (Z, PIECE, 2 * KV_WIDTH)
    return pl.pallas_call(
        functools.partial(sum_plane_kernel, slots),
        out_shape=jax.ShapeDtypeStruct(shape, BF16),
        in_specs=[SMEM, VMEM],
        out_specs=VMEM,
        scratch_shapes=[pltpu.VMEM(shape, F32)],
        compiler_params=params(16),
    )(plan, parts.reshape(PLANE * slots, PIECE, 2 * KV_WIDTH))


def sum_line_kernel(in_ref, out_ref):
    total = in_ref[0].astype(F32)
    for i in range(1, Z):
        total += in_ref[i].astype(F32)
    out_ref[:, 0, :] = total[:, :KV_WIDTH]
    out_ref[:, 1, :] = total[:, KV_WIDTH:]


def sum_line(parts):
    return pl.pallas_call(
        sum_line_kernel,
        out_shape=jax.ShapeDtypeStruct((PIECE, 2, KV_WIDTH), F32),
        in_specs=[VMEM],
        out_specs=VMEM,
        compiler_params=params(16),
    )(parts)


def slot_index(shape, dim, head, first=0):
    row = (lax.broadcasted_iota(jnp.int32, shape, dim) + first) % SLOTS
    return ((row // LOCAL_ROWS) ^ head) * LOCAL_ROWS + row % LOCAL_ROWS


def attention_kernel(slots, place_ref, packing_ref, lengths_ref, plan_ref, *refs):
    row_refs, prompt_ref, refs = refs[N_HEAD - 1 :: -1], refs[N_HEAD], refs[N_HEAD + 1 :]
    back_refs, grads_ref, refs = refs[:N_HEAD], refs[N_HEAD], refs[N_HEAD + 1 :]
    key_ref, value_ref, weight_ref, dscore_ref = refs

    def rows_of(lo):
        return jnp.concatenate([ref[:, lo : lo + HEAD] for ref in row_refs], axis=0)

    def give_back(block, lo):
        for k, ref in enumerate(back_refs):
            ref[:, lo : lo + HEAD] = block[k * LOCAL_ROWS : (k + 1) * LOCAL_ROWS]

    length = lengths_ref[packing_ref[place_ref[0]]]
    places = slots_of(place_ref, packing_ref, plan_ref, slots)
    key_ref[:PROMPT] = prompt_ref[:, :KV_WIDTH]
    value_ref[:PROMPT] = prompt_ref[:, KV_WIDTH:]
    for g in range(KV_LOCAL):
        cols = slice(g * HEAD, (g + 1) * HEAD)
        key_ref[PROMPT:, cols] = rows_of(2 * Q_WIDTH + g * HEAD)
        value_ref[PROMPT:, cols] = rows_of(2 * Q_WIDTH + KV_WIDTH + g * HEAD)

    width = CHUNK * SLOTS
    head = place_ref[1]
    query_pos = slot_index((1, width), 1, head)
    used = query_pos < length
    strips = [slice(lo, lo + STRIP) for lo in range(0, KEYS, STRIP)]

    def fold(x):
        return jnp.sum(x.reshape(STRIP // 8, 8, width), axis=0)

    def products(g, c):
        cols = slice(g * HEAD, (g + 1) * HEAD)
        at = [(g * PER_GROUP + c * CHUNK + i) * HEAD for i in range(CHUNK)]
        query = jnp.concatenate([rows_of(lo) for lo in at], axis=0)
        out_grad = jnp.concatenate([rows_of(Q_WIDTH + lo) for lo in at], axis=0)
        score = dot(key_ref[:, cols], query, ((1,), (1,)))
        dprob = dot(value_ref[:, cols], out_grad, ((1,), (1,)))
        return query, out_grad, score, dprob

    def softmax(g, c, score, dprob):
        top, scores = None, []
        for strip in strips:
            part = score[strip]
            if strip.start >= PROMPT:
                key_pos = slot_index((STRIP, 1), 0, head, strip.start - PROMPT)
                part = jnp.where(key_pos <= query_pos, part, -jnp.inf)
            scores.append(part)
            most = jnp.max(part.reshape(STRIP // 8, 8, width), axis=0)
            top = most if top is None else jnp.maximum(top, most)
        shift = jnp.max(top, axis=0, keepdims=True) * EXP2_SCALE
        raised, total, moment = [], 0.0, 0.0
        for strip, part in zip(strips, scores):
            part = jnp.exp2(part * EXP2_SCALE - shift)
            raised.append(part)
            total += fold(part)
            moment += fold(part * dprob[strip])
        total = jnp.sum(total, axis=0, keepdims=True)
        moment = jnp.sum(moment, axis=0, keepdims=True)
        scale = jnp.where(used, 1.0 / total, 0.0)
        delta = moment * scale
        here = slice(c * width, (c + 1) * width)
        for strip, part in zip(strips, raised):
            weight = part * scale
            weight_ref[g, strip, here] = weight.astype(BF16)
            dscore_ref[g, strip, here] = (weight * (dprob[strip] - delta)).astype(BF16)

    def query_side(g, c):
        keys_down = key_ref[:, g * HEAD : (g + 1) * HEAD].T
        grad = dot(keys_down, dscore_ref[g, :, c * width : (c + 1) * width], ((1,), (0,)))
        grad = (grad * INV_ROOT).astype(BF16).T
        for i in range(CHUNK):
            give_back(grad[i * SLOTS : (i + 1) * SLOTS], (g * PER_GROUP + c * CHUNK + i) * HEAD)

    def key_side(g, queries, out_grads):
        key_grad = dot(dscore_ref[g], jnp.concatenate(queries, axis=0), ((1,), (0,))) * INV_ROOT
        value_grad = dot(weight_ref[g], jnp.concatenate(out_grads, axis=0), ((1,), (0,)))
        for slot, grad in enumerate((key_grad, value_grad)):
            grad = grad.astype(BF16)
            lo = slot * KV_WIDTH + g * HEAD
            for j, at in enumerate(places):
                grads_ref[at, :, lo : lo + HEAD] = grad[j * PIECE : (j + 1) * PIECE]
            give_back(grad[PROMPT:], Q_WIDTH + lo)

    chunks = [(g, c) for g in range(KV_LOCAL) for c in range(PER_GROUP // CHUNK)]
    ready = {}

    def after(g, c):
        query_side(g, c)
        if c == PER_GROUP // CHUNK - 1:
            done = [ready[g, i] for i in range(c + 1)]
            key_side(g, [x[0] for x in done], [x[1] for x in done])

    for n in range(min(AHEAD, len(chunks))):
        ready[chunks[n]] = products(*chunks[n])
    for n, chunk in enumerate(chunks):
        if n + AHEAD < len(chunks):
            ready[chunks[n + AHEAD]] = products(*chunks[n + AHEAD])
        if AHEAD == 0:
            ready[chunk] = products(*chunk)
        softmax(*chunk, *ready[chunk][2:])
        if n >= BEHIND:
            after(*chunks[n - BEHIND])
    for chunk in chunks[len(chunks) - BEHIND :]:
        after(*chunk)


def attention(place, packing, lengths, plan, rows, prompt, slots):
    flops = 2 * 5 * KEYS * Q_WIDTH // HEAD * SLOTS * HEAD
    block = jax.ShapeDtypeStruct((LOCAL_ROWS, OUT_WIDTH), BF16)
    *back, grads = pl.pallas_call(
        functools.partial(attention_kernel, slots),
        out_shape=(block,) * N_HEAD
        + (jax.ShapeDtypeStruct((PLANE * slots, PIECE, 2 * KV_WIDTH), BF16),),
        in_specs=[SMEM] * 4 + [VMEM] * (N_HEAD + 1),
        out_specs=(VMEM,) * (N_HEAD + 1),
        scratch_shapes=[
            pltpu.VMEM((KEYS, KV_WIDTH), BF16),
            pltpu.VMEM((KEYS, KV_WIDTH), BF16),
            pltpu.VMEM((KV_LOCAL, KEYS, PER_GROUP * SLOTS), BF16),
            pltpu.VMEM((KV_LOCAL, KEYS, PER_GROUP * SLOTS), BF16),
        ],
        compiler_params=params(32),
        cost_estimate=pl.CostEstimate(
            flops=flops, bytes_accessed=6 * 2**20, transcendentals=KEYS * SLOTS * 16
        ),
    )(place, packing, lengths, plan, *reversed(rows), prompt)
    return back, grads.reshape(PLANE, slots * PIECE, 2 * KV_WIDTH)


def exchange(parts, axes):
    return lax.all_to_all(parts, axes, split_axis=0, concat_axis=0, tiled=True)


def swap(blocks):
    blocks = list(blocks)
    for k in reversed(range(1, N_HEAD)):
        pairs = [(i, i ^ k) for i in range(N_HEAD)]
        blocks[k] = lax.ppermute(blocks[k], ("xh", "c"), pairs)
    return blocks


def shards(queries, out_grads, response_kv, prompt_kv, packing, lengths, owner):
    place = jnp.stack([lax.axis_index(("xl", "z", "y")), lax.axis_index(("xh", "c"))])
    place = place.astype(jnp.int32)
    plane = ("xl", "y")
    *rows, line = pack(queries, out_grads, response_kv, prompt_kv)
    line = exchange(line, "z")
    plan = make_plan(place, packing, owner)
    rows = swap(rows)

    def gather(slots, line):
        parts = exchange(select(plan, line, slots), plane)
        return collect(place, packing, plan, parts, slots)

    def reduce(slots, prompt, *rows):
        back, grads = attention(place, packing, lengths, plan, rows, prompt, slots)
        return back, sum_plane(plan, exchange(grads, plane), slots)

    choice = plan[CHOICE, 0]
    prompt = lax.switch(
        choice, [functools.partial(gather, slots) for slots in SLOT_COUNTS], line
    )
    back, grads = lax.switch(
        choice, [functools.partial(reduce, slots) for slots in SLOT_COUNTS], prompt, *rows
    )
    grads = exchange(grads, "z")
    back = swap(back)
    query_grad, resp_grad = unpack_rows(place, back)
    return query_grad, resp_grad, sum_line(grads)


def solution(mesh):
    fine = Mesh(mesh.devices.reshape(X_LO, Z, Y, 2, 2), ("xl", "z", "y", "xh", "c"))
    seq, head = ("xl", "z", "y"), ("xh", "c")
    return jax.shard_map(
        shards,
        mesh=fine,
        in_specs=(
            P(seq + head, None),
            P(seq + head, None),
            P(seq + head, None, None),
            P(seq, None, head),
            P(),
            P(),
            P(),
        ),
        out_specs=(
            P(seq + head, None),
            P(seq + head, None, None),
            P(seq, None, head),
        ),
        check_vma=False,
    )
```

```python
import functools
import math

import jax
import jax.numpy as jnp
from jax import lax
from jax.experimental import pallas as pl
from jax.experimental.pallas import tpu as pltpu
from jax.sharding import Mesh
from jax.sharding import PartitionSpec as P

QUERY_HEADS = 64
KEY_VALUE_HEADS = 8
HEAD = 128
GROUP = 16
PIECE = 16
PROMPT = GROUP * PIECE
SLOTS = 128
KEYS = PROMPT + SLOTS
X_LO, Z, Y = 2, 16, 4
PLANE = X_LO * Y
N_SEQ = PLANE * Z
SLOT_COUNTS = (4, 5, 6, 7, 8, GROUP)
N_HEAD = 4
LOCAL_ROWS = SLOTS // N_HEAD
KV_LOCAL = KEY_VALUE_HEADS // N_HEAD
PER_GROUP = QUERY_HEADS // KEY_VALUE_HEADS
Q_WIDTH = KV_LOCAL * PER_GROUP * HEAD
KV_WIDTH = KV_LOCAL * HEAD
IN_WIDTH = 2 * Q_WIDTH + 2 * KV_WIDTH
OUT_WIDTH = Q_WIDTH + 2 * KV_WIDTH
CHUNK, STRIP, AHEAD, BEHIND = 8, 64, 1, 1
INV_ROOT = 1.0 / math.sqrt(HEAD)
EXP2_SCALE = INV_ROOT / math.log(2.0)

BF16 = jnp.bfloat16
F32 = jnp.float32
PLACE, SOURCE, COUNT, CHOICE = range(4)

SMEM = pl.BlockSpec(memory_space=pltpu.SMEM)
VMEM = pl.BlockSpec(memory_space=pltpu.VMEM)


def params(mib):
    return pltpu.CompilerParams(vmem_limit_bytes=mib * 2**20)


def dot(a, b, contract):
    return lax.dot_general(a, b, (contract, ((), ())), preferred_element_type=F32)


def line_of(s):
    return ((s >> 6) << 2) | (s & 3)


def height_of(s):
    return (s >> 2) & 15


def plan_kernel(place_ref, packing_ref, owner_ref, plan_ref):
    me = place_ref[0]
    square = (N_SEQ, N_SEQ)
    lane = lax.broadcasted_iota(jnp.int32, square, 1)
    row = lax.broadcasted_iota(jnp.int32, square, 0)
    across = jnp.broadcast_to(owner_ref[...], square)
    down = across.T
    same = (line_of(down) == line_of(across)) & ((row >> 4) == (lane >> 4))
    ones = same.astype(jnp.int32)
    most = jnp.max(jnp.sum(ones, axis=0, keepdims=True), axis=1, keepdims=True)
    rank = jnp.sum(jnp.where(row < lane, ones, 0), axis=0, keepdims=True)
    plan_ref[PLACE : PLACE + 1, :] = line_of(owner_ref[...]) * GROUP + rank
    rank_down = jnp.sum(jnp.where(lane < row, ones, 0), axis=1, keepdims=True)
    wanted = jnp.zeros((1, N_SEQ), jnp.int32)
    for d in range(PLANE):
        there = (d // Y) * (Z * Y) + height_of(me) * Y + d % Y
        wanted = jnp.where((lane[:1] >> 4) == d, packing_ref[there] >> 4, wanted)
    held = ((row >> 4) == wanted) & (line_of(down) == line_of(me))
    found = held & (rank_down == (lane & 15))
    plan_ref[SOURCE : SOURCE + 1, :] = jnp.sum(
        jnp.where(found, height_of(down), 0), axis=0, keepdims=True
    )
    plan_ref[COUNT : COUNT + 1, :] = jnp.sum(held.astype(jnp.int32), axis=0, keepdims=True)
    choice = sum((most > n).astype(jnp.int32) for n in SLOT_COUNTS[:-1])
    plan_ref[CHOICE : CHOICE + 1, :] = jnp.broadcast_to(choice, (1, N_SEQ))


def make_plan(place, packing, owner):
    return pl.pallas_call(
        plan_kernel,
        out_shape=jax.ShapeDtypeStruct((4, N_SEQ), jnp.int32),
        in_specs=[SMEM, SMEM, VMEM],
        out_specs=VMEM,
    )(place, packing, owner.reshape(1, N_SEQ))


def select_kernel(slots, plan_ref, line_ref, out_ref):
    for d in range(PLANE):
        for c in range(slots):
            out_ref[d * slots + c] = line_ref[plan_ref[SOURCE, d * GROUP + c]]


def select(plan, line, slots):
    out = pl.pallas_call(
        functools.partial(select_kernel, slots),
        out_shape=jax.ShapeDtypeStruct((PLANE * slots, PIECE, 2 * KV_WIDTH), BF16),
        in_specs=[SMEM, VMEM],
        out_specs=VMEM,
        compiler_params=params(16),
    )(plan, line)
    return out.reshape(PLANE, slots * PIECE, 2 * KV_WIDTH)


def pack_kernel(q_ref, g_ref, kv_ref, piece_ref, *refs):
    row_refs, line_ref, kv_here, piece_here, line_here, sems = refs[:N_HEAD], *refs[N_HEAD:]
    fetch_piece = pltpu.make_async_copy(piece_ref, piece_here, sems.at[0])
    fetch_kv = pltpu.make_async_copy(kv_ref, kv_here, sems.at[1])
    store_line = pltpu.make_async_copy(line_here, line_ref, sems.at[2])
    fetch_piece.start()
    fetch_kv.start()
    head = lax.axis_index("xh") * 2 + lax.axis_index("c")
    others = [head ^ k for k in range(N_HEAD)]
    fetches = []
    for k in reversed(range(N_HEAD)):
        wide = pl.ds(pl.multiple_of(others[k] * Q_WIDTH, Q_WIDTH), Q_WIDTH)
        for i, ref in enumerate((q_ref, g_ref)):
            here = row_refs[k].at[:, i * Q_WIDTH : (i + 1) * Q_WIDTH]
            fetches.append(pltpu.make_async_copy(ref.at[:, wide], here, sems.at[3 + 2 * k + i]))
            fetches[-1].start()
    fetch_piece.wait()
    flat = jnp.concatenate([piece_here[:, 0, :], piece_here[:, 1, :]], axis=1)
    for z in range(Z):
        line_here[z] = flat
    store_line.start()
    fetch_kv.wait()
    for other, out_ref in zip(others, row_refs):
        narrow = pl.ds(pl.multiple_of(other * KV_WIDTH, KV_WIDTH), KV_WIDTH)
        for i in range(2):
            lo = 2 * Q_WIDTH + i * KV_WIDTH
            out_ref[:, lo : lo + KV_WIDTH] = kv_here[:, i, narrow]
    for fetch in fetches:
        fetch.wait()
    store_line.wait()


def pack(queries, grads, kv, piece):
    args = [pltpu.with_memory_space_constraint(x, pltpu.HBM) for x in (queries, grads, kv, piece)]
    line = jax.ShapeDtypeStruct((Z, PIECE, 2 * KV_WIDTH), BF16)
    hbm = pl.BlockSpec(memory_space=pltpu.HBM)
    return pl.pallas_call(
        pack_kernel,
        out_shape=(jax.ShapeDtypeStruct((LOCAL_ROWS, IN_WIDTH), BF16),) * N_HEAD + (line,),
        in_specs=[hbm] * 4,
        out_specs=(VMEM,) * N_HEAD + (hbm,),
        scratch_shapes=[
            pltpu.VMEM(kv.shape, BF16),
            pltpu.VMEM(piece.shape, BF16),
            pltpu.VMEM(line.shape, BF16),
            pltpu.SemaphoreType.DMA((3 + 2 * N_HEAD,)),
        ],
        compiler_params=params(16),
    )(*args)


def unpack_kernel(place_ref, *refs):
    q_ref, kv_ref = refs[N_HEAD:]
    for k, in_ref in enumerate(refs[N_HEAD - 1 :: -1]):
        other = place_ref[1] ^ k
        wide = pl.ds(pl.multiple_of(other * Q_WIDTH, Q_WIDTH), Q_WIDTH)
        narrow = pl.ds(pl.multiple_of(other * KV_WIDTH, KV_WIDTH), KV_WIDTH)
        q_ref[:, wide] = in_ref[:, :Q_WIDTH]
        kv_ref[:, 0, narrow] = in_ref[:, Q_WIDTH : Q_WIDTH + KV_WIDTH]
        kv_ref[:, 1, narrow] = in_ref[:, Q_WIDTH + KV_WIDTH :]


def unpack_rows(place, blocks):
    return pl.pallas_call(
        unpack_kernel,
        out_shape=(
            jax.ShapeDtypeStruct((LOCAL_ROWS, N_HEAD * Q_WIDTH), BF16),
            jax.ShapeDtypeStruct((LOCAL_ROWS, 2, N_HEAD * KV_WIDTH), BF16),
        ),
        in_specs=[SMEM] + [VMEM] * N_HEAD,
        out_specs=(VMEM, VMEM),
        compiler_params=params(16),
    )(place, *reversed(blocks))


def slots_of(place_ref, packing_ref, plan_ref, slots):
    first = (packing_ref[place_ref[0]] >> 4) << 4
    places = [plan_ref[PLACE, first + j] for j in range(GROUP)]
    return [(place >> 4) * slots + (place & 15) for place in places]


def collect_kernel(slots, place_ref, packing_ref, plan_ref, parts_ref, out_ref):
    for j, at in enumerate(slots_of(place_ref, packing_ref, plan_ref, slots)):
        out_ref[j * PIECE : (j + 1) * PIECE] = parts_ref[at]


def collect(place, packing, plan, parts, slots):
    return pl.pallas_call(
        functools.partial(collect_kernel, slots),
        out_shape=jax.ShapeDtypeStruct((PROMPT, 2 * KV_WIDTH), BF16),
        in_specs=[SMEM, SMEM, SMEM, VMEM],
        out_specs=VMEM,
        compiler_params=params(16),
    )(place, packing, plan, parts.reshape(PLANE * slots, PIECE, 2 * KV_WIDTH))


def sum_plane_kernel(slots, plan_ref, part_ref, out_ref, total_ref):
    total_ref[...] = jnp.zeros_like(total_ref)
    for d in range(PLANE):

        @pl.loop(0, plan_ref[COUNT, d * GROUP])
        def _(c, d=d):
            z = plan_ref[SOURCE, d * GROUP + c]
            total_ref[z] = total_ref[z] + part_ref[d * slots + c].astype(F32)

    out_ref[...] = total_ref[...].astype(BF16)


def sum_plane(plan, parts, slots):
    shape = (Z, PIECE, 2 * KV_WIDTH)
    return pl.pallas_call(
        functools.partial(sum_plane_kernel, slots),
        out_shape=jax.ShapeDtypeStruct(shape, BF16),
        in_specs=[SMEM, VMEM],
        out_specs=VMEM,
        scratch_shapes=[pltpu.VMEM(shape, F32)],
        compiler_params=params(16),
    )(plan, parts.reshape(PLANE * slots, PIECE, 2 * KV_WIDTH))


def sum_line_kernel(in_ref, out_ref):
    total = in_ref[0].astype(F32)
    for i in range(1, Z):
        total += in_ref[i].astype(F32)
    out_ref[:, 0, :] = total[:, :KV_WIDTH]
    out_ref[:, 1, :] = total[:, KV_WIDTH:]


def sum_line(parts):
    return pl.pallas_call(
        sum_line_kernel,
        out_shape=jax.ShapeDtypeStruct((PIECE, 2, KV_WIDTH), F32),
        in_specs=[VMEM],
        out_specs=VMEM,
        compiler_params=params(16),
    )(parts)


def slot_index(shape, dim, head, first=0):
    row = (lax.broadcasted_iota(jnp.int32, shape, dim) + first) % SLOTS
    return ((row // LOCAL_ROWS) ^ head) * LOCAL_ROWS + row % LOCAL_ROWS


def attention_kernel(slots, place_ref, packing_ref, lengths_ref, plan_ref, *refs):
    row_refs, prompt_ref, refs = refs[N_HEAD - 1 :: -1], refs[N_HEAD], refs[N_HEAD + 1 :]
    back_refs, grads_ref, refs = refs[:N_HEAD], refs[N_HEAD], refs[N_HEAD + 1 :]
    key_ref, value_ref, weight_ref, dscore_ref = refs

    def rows_of(lo):
        return jnp.concatenate([ref[:, lo : lo + HEAD] for ref in row_refs], axis=0)

    def give_back(block, lo):
        for k, ref in enumerate(back_refs):
            ref[:, lo : lo + HEAD] = block[k * LOCAL_ROWS : (k + 1) * LOCAL_ROWS]

    length = lengths_ref[packing_ref[place_ref[0]]]
    places = slots_of(place_ref, packing_ref, plan_ref, slots)
    key_ref[:PROMPT] = prompt_ref[:, :KV_WIDTH]
    value_ref[:PROMPT] = prompt_ref[:, KV_WIDTH:]
    for g in range(KV_LOCAL):
        cols = slice(g * HEAD, (g + 1) * HEAD)
        key_ref[PROMPT:, cols] = rows_of(2 * Q_WIDTH + g * HEAD)
        value_ref[PROMPT:, cols] = rows_of(2 * Q_WIDTH + KV_WIDTH + g * HEAD)

    width = CHUNK * SLOTS
    head = place_ref[1]
    query_pos = slot_index((1, width), 1, head)
    used = query_pos < length
    strips = [slice(lo, lo + STRIP) for lo in range(0, KEYS, STRIP)]

    def fold(x):
        return jnp.sum(x.reshape(STRIP // 8, 8, width), axis=0)

    def products(g, c):
        cols = slice(g * HEAD, (g + 1) * HEAD)
        at = [(g * PER_GROUP + c * CHUNK + i) * HEAD for i in range(CHUNK)]
        query = jnp.concatenate([rows_of(lo) for lo in at], axis=0)
        out_grad = jnp.concatenate([rows_of(Q_WIDTH + lo) for lo in at], axis=0)
        score = dot(key_ref[:, cols], query, ((1,), (1,)))
        dprob = dot(value_ref[:, cols], out_grad, ((1,), (1,)))
        return query, out_grad, score, dprob

    def softmax(g, c, score, dprob):
        top, scores = None, []
        for strip in strips:
            part = score[strip]
            if strip.start >= PROMPT:
                key_pos = slot_index((STRIP, 1), 0, head, strip.start - PROMPT)
                part = jnp.where(key_pos <= query_pos, part, -jnp.inf)
            scores.append(part)
            most = jnp.max(part.reshape(STRIP // 8, 8, width), axis=0)
            top = most if top is None else jnp.maximum(top, most)
        shift = jnp.max(top, axis=0, keepdims=True) * EXP2_SCALE
        raised, total, moment = [], 0.0, 0.0
        for strip, part in zip(strips, scores):
            part = jnp.exp2(part * EXP2_SCALE - shift)
            raised.append(part)
            total += fold(part)
            moment += fold(part * dprob[strip])
        total = jnp.sum(total, axis=0, keepdims=True)
        moment = jnp.sum(moment, axis=0, keepdims=True)
        scale = jnp.where(used, 1.0 / total, 0.0)
        delta = moment * scale
        here = slice(c * width, (c + 1) * width)
        for strip, part in zip(strips, raised):
            weight = part * scale
            weight_ref[g, strip, here] = weight.astype(BF16)
            dscore_ref[g, strip, here] = (weight * (dprob[strip] - delta)).astype(BF16)

    def query_side(g, c):
        keys_down = key_ref[:, g * HEAD : (g + 1) * HEAD].T
        grad = dot(keys_down, dscore_ref[g, :, c * width : (c + 1) * width], ((1,), (0,)))
        grad = (grad * INV_ROOT).astype(BF16).T
        for i in range(CHUNK):
            give_back(grad[i * SLOTS : (i + 1) * SLOTS], (g * PER_GROUP + c * CHUNK + i) * HEAD)

    def key_side(g, queries, out_grads):
        key_grad = dot(dscore_ref[g], jnp.concatenate(queries, axis=0), ((1,), (0,))) * INV_ROOT
        value_grad = dot(weight_ref[g], jnp.concatenate(out_grads, axis=0), ((1,), (0,)))
        for slot, grad in enumerate((key_grad, value_grad)):
            grad = grad.astype(BF16)
            lo = slot * KV_WIDTH + g * HEAD
            for j, at in enumerate(places):
                grads_ref[at, :, lo : lo + HEAD] = grad[j * PIECE : (j + 1) * PIECE]
            give_back(grad[PROMPT:], Q_WIDTH + lo)

    chunks = [(g, c) for g in range(KV_LOCAL) for c in range(PER_GROUP // CHUNK)]
    ready = {}

    def after(g, c):
        query_side(g, c)
        if c == PER_GROUP // CHUNK - 1:
            done = [ready[g, i] for i in range(c + 1)]
            key_side(g, [x[0] for x in done], [x[1] for x in done])

    for n in range(min(AHEAD, len(chunks))):
        ready[chunks[n]] = products(*chunks[n])
    for n, chunk in enumerate(chunks):
        if n + AHEAD < len(chunks):
            ready[chunks[n + AHEAD]] = products(*chunks[n + AHEAD])
        if AHEAD == 0:
            ready[chunk] = products(*chunk)
        softmax(*chunk, *ready[chunk][2:])
        if n >= BEHIND:
            after(*chunks[n - BEHIND])
    for chunk in chunks[len(chunks) - BEHIND :]:
        after(*chunk)


def attention(place, packing, lengths, plan, rows, prompt, slots):
    flops = 2 * 5 * KEYS * Q_WIDTH // HEAD * SLOTS * HEAD
    block = jax.ShapeDtypeStruct((LOCAL_ROWS, OUT_WIDTH), BF16)
    *back, grads = pl.pallas_call(
        functools.partial(attention_kernel, slots),
        out_shape=(block,) * N_HEAD
        + (jax.ShapeDtypeStruct((PLANE * slots, PIECE, 2 * KV_WIDTH), BF16),),
        in_specs=[SMEM] * 4 + [VMEM] * (N_HEAD + 1),
        out_specs=(VMEM,) * (N_HEAD + 1),
        scratch_shapes=[
            pltpu.VMEM((KEYS, KV_WIDTH), BF16),
            pltpu.VMEM((KEYS, KV_WIDTH), BF16),
            pltpu.VMEM((KV_LOCAL, KEYS, PER_GROUP * SLOTS), BF16),
            pltpu.VMEM((KV_LOCAL, KEYS, PER_GROUP * SLOTS), BF16),
        ],
        compiler_params=params(32),
        cost_estimate=pl.CostEstimate(
            flops=flops, bytes_accessed=6 * 2**20, transcendentals=KEYS * SLOTS * 16
        ),
    )(place, packing, lengths, plan, *reversed(rows), prompt)
    return back, grads.reshape(PLANE, slots * PIECE, 2 * KV_WIDTH)


def exchange(parts, axes):
    return lax.all_to_all(parts, axes, split_axis=0, concat_axis=0, tiled=True)


def swap(blocks):
    blocks = list(blocks)
    for k in reversed(range(1, N_HEAD)):
        pairs = [(i, i ^ k) for i in range(N_HEAD)]
        blocks[k] = lax.ppermute(blocks[k], ("xh", "c"), pairs)
    return blocks


def shards(queries, out_grads, response_kv, prompt_kv, packing, lengths, owner):
    place = jnp.stack([lax.axis_index(("xl", "z", "y")), lax.axis_index(("xh", "c"))])
    place = place.astype(jnp.int32)
    plane = ("xl", "y")
    *rows, line = pack(queries, out_grads, response_kv, prompt_kv)
    line = exchange(line, "z")
    plan = make_plan(place, packing, owner)
    rows = swap(rows)

    def gather(slots, line):
        parts = exchange(select(plan, line, slots), plane)
        return collect(place, packing, plan, parts, slots)

    def reduce(slots, prompt, *rows):
        back, grads = attention(place, packing, lengths, plan, rows, prompt, slots)
        return back, sum_plane(plan, exchange(grads, plane), slots)

    choice = plan[CHOICE, 0]
    prompt = lax.switch(
        choice, [functools.partial(gather, slots) for slots in SLOT_COUNTS], line
    )
    back, grads = lax.switch(
        choice, [functools.partial(reduce, slots) for slots in SLOT_COUNTS], prompt, *rows
    )
    grads = exchange(grads, "z")
    back = swap(back)
    query_grad, resp_grad = unpack_rows(place, back)
    return query_grad, resp_grad, sum_line(grads)


def solution(mesh):
    fine = Mesh(mesh.devices.reshape(X_LO, Z, Y, 2, 2), ("xl", "z", "y", "xh", "c"))
    seq, head = ("xl", "z", "y"), ("xh", "c")
    return jax.shard_map(
        shards,
        mesh=fine,
        in_specs=(
            P(seq + head, None),
            P(seq + head, None),
            P(seq + head, None, None),
            P(seq, None, head),
            P(),
            P(),
            P(),
        ),
        out_specs=(
            P(seq + head, None),
            P(seq + head, None, None),
            P(seq, None, head),
        ),
        check_vma=False,
    )
```
